128 devices in a mesh: rank: 8 (over x_hi, y), expert: 16 (over z, x_lo, core).
Axes of the slice: x: 4 (x_hi: 2, x_lo: 2; x = x_hi * 2 + x_lo), y: 4, z: 4, core: 2. Of those that a mesh axis runs over, the one named last changes fastest.
Arguments:
- hidden_in: bfloat16 [1024, 7168], P(('rank', 'expert')), may hold values from -6 to 6
- routes: int32 [1024, 8], P(('rank', 'expert')), may hold values from 0 to 15, all different within a row; in each aligned block of 8 rows (0 to 7, 8 to 15, ...) at most 5 rows name the same one
- gates: bfloat16 [1024, 8], P(('rank', 'expert')), may hold values from 0.049804688 to 0.59765625
- gate_proj: bfloat16 [16, 7168, 2048], P('expert', None, 'rank'), may hold values from -0.0625 to 0.0625
- up_proj: bfloat16 [16, 7168, 2048], P('expert', None, 'rank'), may hold values from -0.0625 to 0.0625
- down_proj: bfloat16 [16, 2048, 7168], P('expert', 'rank'), may hold values from -0.125 to 0.125
- query: bfloat16 [512, 128, 576], P(('rank', 'expert')), may hold values from -60 to 60
- kv_cache: bfloat16 [512, 1024, 576], P(('rank', 'expert')), may hold values from -6 to 6
- lengths: int32 [512], P(('rank', 'expert')), may hold values from 256 to 1024, as said below
- moving: int32 [128], P(('rank', 'expert')), may hold values from 0 to 3
- pair_mask: int32 [1], replicated, may hold values from 1 to 7
Outputs:
- routed: bfloat16 [1024, 7168], P(('rank', 'expert'))
- attention: bfloat16 [512, 128, 512], P(('rank', 'expert'))
- incoming: bfloat16 [128, 1024, 576], P(('rank', 'expert'))
The draws below stay inside these ranges and needn't reach their ends.
Inputs may be any that keep to these rules, and one draw needn't show every extreme that they name: `routes`: in each aligned block of 8 rows (the tokens of one device) no expert is named by more than 5 rows. `lengths`: some request has length 1024. `moving`: indices among the 4 requests of the device. Rank r sends to and receives from rank r XOR pair_mask[0].
All inputs are finite; a program needn't handle non-finite values.
Results may differ from the reference program's by a relative error of at most 0.005.
Values may be sent and summed in bfloat16 or wider, within the bound.
A program may use at most 192 MiB of HBM per device.

```python
import math
import jax
import jax.numpy as jnp
import numpy as np
from jax import lax

D = 7168
FF = 2048
H = 128
LAT = 512
KV = 576
TOP = 8
EXPERTS = 16
TOK_DEV = 8
REQ_DEV = 4
L = 1024
MIG = 1
CAP = 5
TOKENS = 1024
REQS = 512
MOVES = 128
N_RANK = 8
N_EXPERT = 16


def shared_keys(key):
    return jnp.clip(jax.random.normal(key, (REQS, L, KV), jnp.float32), -6.0, 6.0)


def draw_kv_cache(key, part):
    shared = shared_keys(key)
    return shared.astype(jnp.bfloat16)


def draw_query(key, part):
    key = jax.random.fold_in(key, 5)
    noise_key = jax.random.fold_in(key, 0)
    values = jax.random.normal(noise_key, (REQS, H, KV), jnp.float32)
    return jnp.clip(values, -60.0, 60.0).astype(jnp.bfloat16)


def draw_lengths(key, part):
    key = jax.random.fold_in(key, 7)
    drawn = jax.random.randint(key, (REQS,), L // 4, L + 1)
    return drawn.at[0].set(L).astype(jnp.int32)


def place_ends(values, rng, least, largest):
    dims = values.shape
    spot = [jax.random.randint(jax.random.fold_in(rng, axis), (), 0, dims[axis]) for axis in range(len(dims))]
    values = values.at[tuple(spot)].set(least)
    longest = dims.index(max(dims))
    spot[longest] = (spot[longest] + 1) % dims[longest]
    return values.at[tuple(spot)].set(largest)


def shard_levels(key, shape, cuts, smallest, largest):
    loudness = 1.0
    for axis_at, blocks in cuts:
        heights = jax.random.uniform(jax.random.fold_in(jax.random.fold_in(key, 6), axis_at), (blocks,), jnp.float32, smallest / len(cuts), largest / len(cuts))
        loudness = loudness * jnp.repeat(jnp.exp(heights), shape[axis_at] // blocks).reshape((-1,) + (1,) * (len(shape) - 1 - axis_at))
    return loudness


def shared_out(stream_key, own, number, rows, amount, top, reach, skew):
    order = jax.random.permutation(stream_key, amount)
    crowded, common = portions_of(amount, rows * top, reach, skew, True), portions_of(amount, rows * top, reach, skew, False)
    places = jnp.arange(amount)

    def named(sizes, rotation):
        used = int((sizes > 0).sum())
        fixed = max(1, used // 4)
        moved = fixed + (places - fixed + rotation * (used - fixed)) % max(1, amount - fixed)
        return jnp.zeros((amount,), jnp.int32).at[order[jnp.where(places < fixed, places, moved)]].set(jnp.asarray(sizes, jnp.int32))

    sizes = jnp.where(number % 4 == 0, named(crowded, number // 4), named(common, number - number // 4 - 1))
    mixed = jax.random.permutation(jax.random.fold_in(own, 3), amount)
    source_of, receiver = mixed[0:amount // 2 * 2:2], mixed[1:amount // 2 * 2:2]
    slack = jnp.minimum(sizes[source_of] - 1, reach - sizes[receiver]) // 2
    slack = jnp.where((source_of == order[0]) | (receiver == order[0]) | (sizes[receiver] == 0), 0, jnp.maximum(slack, 0))
    moved = jax.random.randint(jax.random.fold_in(own, 4), (amount // 2,), 0, 1 << 20) % (slack + 1)
    sizes = sizes.at[source_of].add(-moved).at[receiver].add(moved)
    items = jnp.searchsorted(jnp.cumsum(sizes), jnp.arange(rows * top), side="right").astype(jnp.int32)
    grid = items.reshape(top, rows).T
    grid = grid[jax.random.permutation(jax.random.fold_in(own, 1), rows)]
    rotation = jax.random.randint(jax.random.fold_in(own, 2), (rows, 1), 0, top)
    return jnp.take_along_axis(grid, (jnp.arange(top)[None, :] + rotation) % top, axis=1)


def portions_of(count, total, most, lean, full):
    portions = [(1 << 20) // math.isqrt(rank ** lean) + 1 for rank in range(1, count + 1)]
    largest = most if full else min(most, max(-(-total // count), total * portions[0] // sum(portions)))
    least = 1 if total - largest >= count - 1 else 0
    given, surplus = [largest] + [least] * (count - 1), total - largest - least * (count - 1)
    while surplus > 0:
        free = [i for i in range(1, count) if given[i] < largest] or [i for i in range(1, count) if given[i] < most]
        mass, remaining = sum([portions[i] for i in free]), surplus
        for i in free:
            more = min(most - given[i], max(1, remaining * portions[i] // mass), surplus)
            given[i] = given[i] + more
            surplus = surplus - more
    return np.array(given)


def noise(key, shape, deviation, most, cuts=(), held_as=jnp.bfloat16):
    array = deviation * jax.random.normal(key, shape, jnp.float32)
    if cuts:
        array = array * shard_levels(key, shape, cuts, -0.22, 0.18)
    return jnp.clip(array, -most, most).astype(held_as)


def setup_inputs(seed: int = 0) -> dict:
    seeds = jax.random.split(jax.random.key(seed), 12)
    hidden_in = noise(seeds[0], (TOKENS, D), 1.0, 6.0, ((0, 128),))
    routes_keys = jax.random.split(jax.random.fold_in(seeds[1], 1), TOKENS // TOK_DEV)
    routes_turns = jax.random.permutation(jax.random.fold_in(seeds[1], 3), TOKENS // TOK_DEV)
    routes = jax.vmap(lambda own, number: shared_out(jax.random.fold_in(seeds[1], 2), own, number, TOK_DEV, EXPERTS, TOP, CAP, 2))(routes_keys, routes_turns).reshape((TOKENS, TOP))
    gates = jnp.clip(0.049804688 + 0.54785156 * jax.random.uniform(seeds[2], (TOKENS, TOP), jnp.float32) ** shard_levels(seeds[2], (TOKENS, TOP), ((0, 128),), -0.2, 0.2), 0.049804688, 0.59765625).astype(jnp.bfloat16)
    gate_proj = noise(seeds[3], (EXPERTS, D, FF), D ** -0.5, 0.0625, ((0, 16), (2, 8)))
    up_proj = noise(seeds[4], (EXPERTS, D, FF), D ** -0.5, 0.0625, ((0, 16), (2, 8)))
    down_proj = noise(seeds[5], (EXPERTS, FF, D), FF ** -0.5, 0.125, ((0, 16), (1, 8)))
    query = draw_query(jax.random.fold_in(seeds[11], 71), 0)
    kv_cache = draw_kv_cache(jax.random.fold_in(seeds[11], 71), 0)
    lengths = draw_lengths(jax.random.fold_in(seeds[11], 71), 0)
    moving = place_ends(jax.random.randint(seeds[9], (MOVES,), 0, REQ_DEV), jax.random.fold_in(seeds[9], 1), 0, REQ_DEV - 1).astype(jnp.int32)
    pair_mask = jax.random.randint(seeds[10], (1,), 1, N_RANK).astype(jnp.int32)
    return dict(hidden_in=hidden_in, routes=routes, gates=gates, gate_proj=gate_proj, up_proj=up_proj, down_proj=down_proj, query=query, kv_cache=kv_cache, lengths=lengths, moving=moving, pair_mask=pair_mask)


score_scale = 192.0 ** -0.5


def expert_block(inputs, w_gate, w_up, w_down):
    wide_in = inputs.astype(jnp.float32)
    gate_part = jnp.dot(wide_in, w_gate.astype(jnp.float32))
    up_part = jnp.dot(wide_in, w_up.astype(jnp.float32))
    hidden = (jax.nn.silu(gate_part) * up_part).astype(jnp.bfloat16)
    return jnp.dot(hidden.astype(jnp.float32), w_down.astype(jnp.float32))


def attend_packed(packed):
    query_one, cache_one, length_one = packed
    cache_wide = cache_one.astype(jnp.float32)
    scores = jnp.dot(query_one.astype(jnp.float32), cache_wide.T) * score_scale
    is_valid = jnp.arange(L, dtype=jnp.int32) < length_one
    scores = jnp.where(is_valid[None, :], scores, jnp.float32(-1e30))
    row_max = jnp.max(scores, axis=-1, keepdims=True)
    weights = jnp.where(is_valid[None, :], jnp.exp(scores - row_max), jnp.float32(0.0))
    denominator = jnp.sum(weights, axis=-1, keepdims=True)
    rounded = weights.astype(jnp.bfloat16)
    mixed = jnp.dot(rounded.astype(jnp.float32), cache_wide[:, :LAT])
    return (mixed / denominator).astype(jnp.bfloat16)


def reference(hidden_in, routes, gates, gate_proj, up_proj, down_proj, query, kv_cache, lengths, moving, pair_mask):
    attention = lax.map(attend_packed, (query, kv_cache, lengths))
    slot_count = (TOKENS // TOK_DEV) * CAP
    expert_ids = jnp.arange(EXPERTS, dtype=jnp.int32)
    named = routes[:, :, None] == expert_ids[None, None, :]
    chosen = jnp.any(named, axis=1)
    weight_table = jnp.sum(jnp.where(named, gates.astype(jnp.float32)[:, :, None], jnp.float32(0.0)), axis=1)

    def one_expert(accumulated, expert_index):
        is_member = chosen[:, expert_index]
        slot_order = jnp.argsort(jnp.where(is_member, 0, 1).astype(jnp.int32), stable=True)[:slot_count].astype(jnp.int32)
        inputs = hidden_in[slot_order]
        w_gate = lax.dynamic_index_in_dim(gate_proj, expert_index, 0, keepdims=False)
        w_up = lax.dynamic_index_in_dim(up_proj, expert_index, 0, keepdims=False)
        w_down = lax.dynamic_index_in_dim(down_proj, expert_index, 0, keepdims=False)
        outputs = expert_block(inputs, w_gate, w_up, w_down)
        slot_scale = weight_table[slot_order, expert_index]
        return accumulated.at[slot_order].add(outputs * slot_scale[:, None]), None

    accumulated, unused = lax.scan(one_expert, jnp.zeros((TOKENS, D), jnp.float32), expert_ids)
    routed = accumulated.astype(jnp.bfloat16)

    device_ids = jnp.arange(N_RANK * N_EXPERT, dtype=jnp.int32)
    rank_of = device_ids // N_EXPERT
    expert_of = device_ids % N_EXPERT
    partner = (jnp.bitwise_xor(rank_of, pair_mask[0]) * N_EXPERT + expert_of).astype(jnp.int32)
    list_index = (partner[:, None] * MIG + jnp.arange(MIG, dtype=jnp.int32)[None, :]).reshape(-1)
    request = (jnp.repeat(partner, MIG) * REQ_DEV + moving[list_index]).astype(jnp.int32)
    moved = kv_cache[request]
    in_length = jnp.arange(L, dtype=jnp.int32)[None, :] < lengths[request][:, None]
    incoming = jnp.where(in_length[:, :, None], moved, jnp.zeros_like(moved))
    return routed, attention, incoming
```

```python
import functools

import jax
import jax.numpy as jnp
from jax import lax
from jax.experimental import pallas as pl
from jax.experimental.pallas import tpu as pltpu
from jax.sharding import PartitionSpec as P

LAT = 512
SCALE = 192.0 ** (-0.5)
MESH = pl.DeviceIdType.MESH
F32 = jnp.float32
BF16 = jnp.bfloat16
GATE_TILE = 128

DIMS = ((1, 0, 2), (2, 1, 0), (0, 2, 1))
GATE_PART = 2


def part_sizes(half):
    if half == 3584:
        return (1536, 1024, 1024)
    return (half // 3,) * 3


def kernel(
    hid_ref, routes_ref, gates_ref, wg_ref, wu_ref, wd_ref, q_ref, kv_ref, len_ref, mov_ref, mask_ref,
    routed_ref, att_ref, inc_ref,
    x0, x1, x2, w, dn, acc, rb, h, gbuf, tmp,
    f3_0, f3_1, f3_2, r3p_0, r3p_1, r3p_2, r3m_0, r3m_1, r3m_2, t2_0, t2_1, t2_2,
    s2_0, s2_1, s2_2, q2_0, q2_1, q2_2, t1_0, t1_1, t1_2, s1_0, s1_1, s1_2, q1_0, q1_1, q1_2,
    stage_s, stage_r, fin, finr, kvv, qv,
    ya1, ya2, za1, za2, va1, va2, ua, sa, yb1, yb2, zb1, zb2, vb1, vb2, ub, sb,
    send_sems, recv_sems, local_sems,
):
    half = hid_ref.shape[1] // 2
    sizes = part_sizes(half)
    starts = (0, sizes[0], sizes[0] + sizes[1])
    xs, f3, r3p, r3m = (x0, x1, x2), (f3_0, f3_1, f3_2), (r3p_0, r3p_1, r3p_2), (r3m_0, r3m_1, r3m_2)
    t2, s2, q2 = (t2_0, t2_1, t2_2), (s2_0, s2_1, s2_2), (q2_0, q2_1, q2_2)
    t1, s1, q1 = (t1_0, t1_1, t1_2), (s1_0, s1_1, s1_2), (q1_0, q1_1, q1_2)
    ff = wg_ref.shape[1]

    r = lax.axis_index("rank")
    e = lax.axis_index("expert")
    c = e % 2
    oc = 1 - c
    y = r % 4
    z = e // 4
    x = (r // 4) * 2 + (e // 2) % 2
    pos = (x, y, z)

    def at_chip(px, py, pz, core):
        return ((px // 2) * 4 + py, pz * 4 + (px % 2) * 2 + core)

    def nb(dim, delta):
        moved = [(v + delta + 4) % 4 if i == dim else v for i, v in enumerate(pos)]
        return at_chip(*moved, c)

    sibling = at_chip(x, y, z, oc)
    y_one = at_chip(x, y + 1 - 2 * (y % 2), z, c)
    y_three = at_chip(x, 3 - y, z, c)

    counter = [0]
    started = []

    def rc(src, dst, device):
        i = counter[0]
        counter[0] += 1
        return pltpu.make_async_remote_copy(
            src_ref=src, dst_ref=dst, send_sem=send_sems.at[i], recv_sem=recv_sems.at[i],
            device_id=device, device_id_type=MESH,
        )

    def go(src, dst, device):
        d = rc(src, dst, device)
        d.start()
        started.append(d)
        return d

    def done_sending():
        for d in started:
            d.wait_send()
        started.clear()

    locals_ = []

    def lc(src, dst):
        d = pltpu.make_async_copy(src, dst, local_sems.at[len(locals_)])
        locals_.append(d)
        d.start()
        return d

    lkv = lc(kv_ref, kvv)
    lq = lc(q_ref, qv)
    mine = pl.ds(pl.multiple_of(c * half, 128), half)
    other = pl.ds(pl.multiple_of(oc * half, 128), half)
    lwg = lc(wg_ref.at[mine, :], w.at[2 * c])
    lwu = lc(wu_ref.at[mine, :], w.at[2 * c + 1])
    lwd = lc(wd_ref.at[:, mine], dn.at[c])

    lane = lax.broadcasted_iota(jnp.int32, (8, GATE_TILE), 1)
    gate_rows = jnp.zeros((8, GATE_TILE), F32)
    wide_gates = gates_ref[...].astype(F32)
    names = routes_ref[...]
    for k in range(routes_ref.shape[1]):
        gate_rows = gate_rows + jnp.where(lane == names[:, k : k + 1], wide_gates[:, k : k + 1], 0.0)
    stage_s[:, pl.ds(0, half)] = hid_ref[:, other]
    stage_s[:, pl.ds(half, GATE_TILE)] = gate_rows.astype(BF16)

    barrier = pltpu.get_barrier_semaphore()
    for device in (nb(0, 1), nb(0, -1), nb(1, 1), nb(1, -1), nb(2, 1), nb(2, -1), sibling):
        pl.semaphore_signal(barrier, inc=1, device_id=device, device_id_type=MESH)
    pl.semaphore_wait(barrier, 7)

    tok = go(stage_s, stage_r, sibling)
    rwg = go(wg_ref.at[other, :], w.at[2 * c], sibling)
    rwu = go(wu_ref.at[other, :], w.at[2 * c + 1], sibling)
    rwd = go(wd_ref.at[:, other], dn.at[c], sibling)

    tok.wait_recv()
    cf = c.astype(F32)
    own_wide = jnp.concatenate([hid_ref[:, mine].astype(F32), gate_rows], axis=1)
    got_wide = stage_r[...].astype(F32)
    top = own_wide * (1.0 - cf) + got_wide * cf
    bottom = got_wide * (1.0 - cf) + own_wide * cf
    block = jnp.concatenate([top, bottom], axis=0).astype(BF16)

    def place(p):
        return tuple(pos[d] for d in DIMS[p])

    def near(v, delta):
        return (v + delta + 4) % 4

    for p in range(3):
        a1, a2, a3 = place(p)
        end = half + GATE_TILE if p == GATE_PART else starts[p] + sizes[p]
        xs[p][a3, a2, a1] = block[:, starts[p] : end]

    g1 = []
    for p in range(3):
        a1, a2, a3 = place(p)
        own = xs[p].at[a3, a2, a1]
        g1.append((go(own, own, nb(DIMS[p][0], 1)), go(own, own, nb(DIMS[p][0], -1))))

    mask = mask_ref[0]
    m_y = mask % 4
    m_x = mask // 4
    sub = ya1.shape[1]
    step_rows = 64 if sub % 64 == 0 else 16

    def for_rows(fn):
        @pl.loop(0, sub // step_rows)
        def _(i):
            fn(pl.ds(pl.multiple_of(i * step_rows, 16), step_rows))

    def pick_rows(dst, dst_slot, part):
        which = mov_ref[0]
        limit = len_ref[which]

        def one(rows):
            first = part * sub + rows.start
            piece = kvv[which, pl.ds(pl.multiple_of(first, 16), step_rows), :].astype(F32)
            at = lax.broadcasted_iota(jnp.int32, piece.shape, 0) + first
            dst[dst_slot, rows, :] = jnp.where(at < limit, piece, 0.0).astype(BF16)

        for_rows(one)

    def move_rows(dst, src, src_slot):
        def one(rows):
            dst[rows, :] = src[src_slot, rows, :]

        for_rows(one)

    def y_first(b1, b2):
        return go(b1.at[0], b1.at[1], y_one), go(b2.at[0], b2.at[1], y_three)

    def y_second(b1, b2, z1, z2, stage, first):
        first[0].wait_recv()
        first[1].wait_recv()
        move_rows(stage.at[0], b1, jnp.where(m_y == 3, 0, 1))
        s3 = go(stage.at[0], z1.at[1], y_three)
        move_rows(stage.at[1], b2, jnp.where(m_y == 1, 0, 1))
        s1_ = go(stage.at[1], z2.at[1], y_one)
        move_rows(z1.at[0], b1, jnp.where(m_y == 1, 1, 0))
        move_rows(z2.at[0], b2, jnp.where(m_y == 3, 1, 0))
        return s3, s1_

    def y_end(z1, z2, second, dst1, dst2):
        second[0].wait_recv()
        second[1].wait_recv()
        move_rows(dst1, z1, jnp.where(m_y <= 1, 0, 1))
        move_rows(dst2, z2, jnp.where((m_y == 0) | (m_y == 3), 0, 1))

    def x_first(v1, v2, u):
        return go(v1.at[0], u.at[0], nb(0, 1)), go(v2.at[0], u.at[1], nb(0, -1))

    def x_second(v1, v2, u, first):
        first[0].wait_recv()
        a = go(u.at[0], v1.at[1], nb(0, 1))
        first[1].wait_recv()
        return a, go(u.at[1], v2.at[1], nb(0, -1))

    def x_end(v1, v2, second, dst1, dst2):
        second[0].wait_recv()
        second[1].wait_recv()
        move_rows(dst1, v1, m_x)
        move_rows(dst2, v2, m_x)

    lkv.wait()
    pick_rows(ya1, 0, 0)
    pick_rows(ya2, 0, 1)
    mig_a = y_first(ya1, ya2)
    pick_rows(vb1, 0, 2)
    pick_rows(vb2, 0, 3)
    mig_b = x_first(vb1, vb2, ub)

    g1f = []
    for p in range(3):
        a1, a2, a3 = place(p)
        cut = xs[p].shape[4] // 256 * 128
        rest = xs[p].shape[4] - cut
        g1[p][0].wait_recv()
        left = xs[p].at[a3, a2, near(a1, -1), :, pl.ds(0, cut)]
        one = go(left, left, nb(DIMS[p][0], 1))
        g1[p][1].wait_recv()
        right = xs[p].at[a3, a2, near(a1, 1), :, pl.ds(cut, rest)]
        g1f.append((one, go(right, right, nb(DIMS[p][0], -1))))

    lq.wait()

    def attend(b):
        kv = kvv[b]
        scores = lax.dot_general(qv[b], kv, (((1,), (1,)), ((), ())), preferred_element_type=F32) * SCALE
        valid = lax.broadcasted_iota(jnp.int32, scores.shape, 1) < len_ref[b]
        scores = jnp.where(valid, scores, -1e30)
        top_score = jnp.max(scores, axis=-1, keepdims=True)
        weights = jnp.where(valid, jnp.exp(scores - top_score), 0.0)
        total = jnp.sum(weights, axis=-1, keepdims=True)
        mixed = jnp.dot(weights.astype(BF16), kv[:, :LAT], preferred_element_type=F32)
        att_ref[b] = (mixed / total).astype(BF16)

    g2, g3 = [], [[None] * 4 for _ in range(3)]
    offs = (0, -1, 1, 2)

    def third(p, k):
        a1, a2, a3 = place(p)
        line = xs[p].at[a3, near(a2, offs[k])]
        g3[p][k] = (go(line, line, nb(DIMS[p][2], 1)), go(line, line, nb(DIMS[p][2], -1)))

    for p in range(3):
        a1, a2, a3 = place(p)
        g1f[p][0].wait_recv()
        g1f[p][1].wait_recv()
        line = xs[p].at[a3, a2]
        g2.append((go(line, line, nb(DIMS[p][1], 1)), go(line, line, nb(DIMS[p][1], -1))))
    for p in range(3):
        third(p, 0)

    @pl.loop(0, 4)
    def _(n):
        for i in range(4):
            for j in range(4):
                acc[n, i, j] = jnp.zeros(acc.shape[3:], F32)

    attend(0)

    g2f = []
    for p in range(3):
        a1, a2, a3 = place(p)
        g2[p][0].wait_recv()
        left = xs[p].at[a3, near(a2, -1), pl.ds(0, 2)]
        one = go(left, left, nb(DIMS[p][1], 1))
        g2[p][1].wait_recv()
        right = xs[p].at[a3, near(a2, 1), pl.ds(2, 2)]
        g2f.append((one, go(right, right, nb(DIMS[p][1], -1))))
        third(p, 1)
        third(p, 2)

    attend(1)
    g3f = [[None] * 4 for _ in range(3)]

    def forward(p, k):
        a1, a2, a3 = place(p)
        g3[p][k][0].wait_recv()
        g3[p][k][1].wait_recv()
        delta = 1 if k % 2 == 0 else -1
        line = xs[p].at[near(a3, -delta), near(a2, offs[k])]
        g3f[p][k] = go(line, line, nb(DIMS[p][2], delta))

    for p in range(3):
        g2f[p][0].wait_recv()
        g2f[p][1].wait_recv()
        third(p, 3)
        forward(p, 0)

    mig_a = y_second(ya1, ya2, za1, za2, sa, mig_a)
    mig_b = x_second(vb1, vb2, ub, mig_b)

    def rows_of(p, j):
        full = slice(None)
        if p == 0:
            return [(i, full, j) for i in range(4)]
        if p == 1:
            return [(j, i, full) for i in range(4)]
        return [(full, j, i) for i in range(4)]

    lwg.wait()
    lwu.wait()
    rwg.wait_recv()
    rwu.wait_recv()

    def project(p, j):
        lhs = xs[p][j][:, :, :, : sizes[p]].reshape(256, sizes[p])

        @pl.loop(0, 4)
        def _(n):
            res = jnp.dot(lhs, w[n, pl.ds(starts[p], sizes[p]), :], preferred_element_type=F32)
            res = res.reshape(4, 4, 16, ff)
            for i, index in enumerate(rows_of(p, j)):
                acc[(n, *index)] = acc[(n, *index)] + res[i]

    for p in range(3):
        project(p, place(p)[2])
    for p in range(3):
        forward(p, 1)
    attend(2)
    for p in range(3):
        forward(p, 2)
    attend(3)
    for p in range(3):
        forward(p, 3)
    for p in range(3):
        project(p, near(place(p)[2], 1))
        project(p, near(place(p)[2], -1))
    y_end(za1, za2, mig_a, va1.at[0], va2.at[0])
    mig_a = x_first(va1, va2, ua)
    x_end(vb1, vb2, mig_b, yb1.at[0], yb2.at[0])
    mig_b = y_first(yb1, yb2)
    for p in range(3):
        for k in range(4):
            g3f[p][k].wait_recv()
        project(p, near(place(p)[2], 2))

    for n in range(2):
        pick = lax.broadcasted_iota(jnp.int32, (GATE_TILE, GATE_TILE), 0) == e - c + n
        pick = jnp.where(pick, 1.0, 0.0).astype(BF16)
        for j in range(4):
            table = xs[GATE_PART][j][:, :, :, sizes[GATE_PART] :].reshape(256, GATE_TILE)
            spread = jnp.dot(table, pick, preferred_element_type=F32).reshape(4, 4, 16, GATE_TILE)
            for i, index in enumerate(rows_of(GATE_PART, j)):
                gbuf[(n, *index)] = spread[i]

    part_sends = []
    for k in (3, 1, 2, 0):
        xx = near(x, offs[k])
        part_sends.append(
            go(acc.at[pl.ds(2 * oc, 2), xx], rb.at[:, xx], sibling)
        )
    hid_sends = []
    for at, k in enumerate((3, 1, 2, 0)):
        xx = near(x, offs[k])
        part_sends[at].wait_recv()
        gate = acc[2 * c, xx] + rb[0, xx]
        up = acc[2 * c + 1, xx] + rb[1, xx]
        h[c, xx] = (gate * (1.0 / (1.0 + jnp.exp(-gate))) * up).astype(BF16)
        hid_sends.append(go(h.at[c, xx], h.at[c, xx], sibling))

    lwd.wait()
    rwd.wait_recv()
    done_sending()
    for d in hid_sends:
        d.wait_recv()

    def down(p, j, dst):
        def pull(ref, n):
            return jnp.concatenate([ref[(n, *i)].reshape(64, ref.shape[-1]) for i in rows_of(p, j)], axis=0)

        hs = [pull(h, n) for n in range(2)]
        gs = [pull(gbuf, n) for n in range(2)]
        gs = [jnp.concatenate([g, g], axis=1) for g in gs]

        @pl.loop(0, sizes[p] // 256)
        def _(n):
            cols = pl.ds(pl.multiple_of(starts[p] + n * 256, 128), 256)
            out = gs[0] * jnp.dot(hs[0], dn[0, :, cols], preferred_element_type=F32)
            out = out + gs[1] * jnp.dot(hs[1], dn[1, :, cols], preferred_element_type=F32)
            dst[:, :, pl.ds(pl.multiple_of(n * 256, 128), 256)] = out.reshape(4, 64, 256)

    roffs = (2, -1, 1, 0)
    fw3 = [[None] * 4 for _ in range(3)]

    def slot(p, which, k):
        return xs[p].at[which, k, :, :, pl.ds(0, sizes[p])]

    def put(p, which, k, value):
        xs[p][which, k, :, :, : sizes[p]] = value.astype(BF16).reshape(4, 16, sizes[p])

    for p in range(3):
        a1, a2, a3 = place(p)
        view = tmp.at[:, :, pl.ds(0, sizes[p])]
        down(p, near(a3, 2), view)
        for k in range(4):
            put(p, 0, k, view[near(a2, roffs[k])])
            fw3[p][k] = go(slot(p, 0, k), f3[p].at[k], nb(DIMS[p][2], 1 if k % 2 == 0 else -1))

    sp, sm = [[None] * 4 for _ in range(3)], [[None] * 4 for _ in range(3)]
    for p in range(3):
        a1, a2, a3 = place(p)
        view = tmp.at[:, :, pl.ds(0, sizes[p])]
        for side, which, sent, back in ((1, 1, sp, r3p), (-1, 2, sm, r3m)):
            down(p, near(a3, side), view)
            summed = (0, 2) if side == 1 else (1, 3)
            alone = (1, 3) if side == 1 else (0, 2)
            for k in alone + summed:
                value = view[near(a2, roffs[k])]
                if k in summed:
                    fw3[p][k].wait_recv()
                    value = value + f3[p][k].reshape(64, sizes[p]).astype(F32)
                put(p, which, k, value)
                sent[p][k] = go(slot(p, which, k), back[p].at[k], nb(DIMS[p][2], side))
    for p in range(3):
        down(p, place(p)[2], t2[p])

    mig_a = x_second(va1, va2, ua, mig_a)
    mig_b = y_second(yb1, yb2, zb1, zb2, sb, mig_b)

    def settle(p, k):
        a1, a2, a3 = place(p)
        sp[p][k].wait_recv()
        sm[p][k].wait_recv()
        got = r3p[p][k].reshape(64, sizes[p]).astype(F32) + r3m[p][k].reshape(64, sizes[p]).astype(F32)
        return t2[p][near(a2, roffs[k])] + got

    fw2 = []
    for p in range(3):
        d = DIMS[p][1]
        s2[p][0] = settle(p, 0).astype(BF16)
        top_half, low_half = pl.ds(0, 32), pl.ds(32, 32)
        fw2.append((
            go(s2[p].at[0, top_half], q2[p].at[0, top_half], nb(d, 1)),
            go(s2[p].at[0, low_half], q2[p].at[0, low_half], nb(d, -1)),
        ))
    back2 = [[None, None] for _ in range(3)]
    for p in range(3):
        d = DIMS[p][1]
        value = settle(p, 1)
        fw2[p][1].wait_recv()
        s2[p][2, pl.ds(0, 32), :] = value[:32].astype(BF16)
        s2[p][2, pl.ds(32, 32), :] = (value[32:] + q2[p][0, pl.ds(32, 32), :].astype(F32)).astype(BF16)
        back2[p][1] = go(s2[p].at[2], q2[p].at[2], nb(d, -1))
    for p in range(3):
        d = DIMS[p][1]
        value = settle(p, 2)
        fw2[p][0].wait_recv()
        s2[p][1, pl.ds(0, 32), :] = (value[:32] + q2[p][0, pl.ds(0, 32), :].astype(F32)).astype(BF16)
        s2[p][1, pl.ds(32, 32), :] = value[32:].astype(BF16)
        back2[p][0] = go(s2[p].at[1], q2[p].at[1], nb(d, 1))

    fw1, back1 = [], []
    for p in range(3):
        a1, a2, a3 = place(p)
        d = DIMS[p][0]
        value = settle(p, 3)
        back2[p][0].wait_recv()
        back2[p][1].wait_recv()
        value = value + q2[p][1].astype(F32) + q2[p][2].astype(F32)
        t1[p][...] = value.reshape(4, 16, sizes[p])
        s1[p][0] = t1[p][near(a1, 2)].astype(BF16)
        cut = sizes[p] // 2
        left, right = pl.ds(0, cut), pl.ds(cut, cut)
        fw1.append((
            go(s1[p].at[0, :, left], q1[p].at[0, :, left], nb(d, 1)),
            go(s1[p].at[0, :, right], q1[p].at[0, :, right], nb(d, -1)),
        ))
    for p in range(3):
        a1, a2, a3 = place(p)
        d = DIMS[p][0]
        cut = sizes[p] // 2
        fw1[p][0].wait_recv()
        value = t1[p][near(a1, 1)]
        s1[p][1, :, pl.ds(0, cut)] = (value[:, :cut] + q1[p][0, :, pl.ds(0, cut)].astype(F32)).astype(BF16)
        s1[p][1, :, pl.ds(cut, cut)] = value[:, cut:].astype(BF16)
        one = go(s1[p].at[1], q1[p].at[1], nb(d, 1))
        fw1[p][1].wait_recv()
        value = t1[p][near(a1, -1)]
        s1[p][2, :, pl.ds(0, cut)] = value[:, :cut].astype(BF16)
        s1[p][2, :, pl.ds(cut, cut)] = (value[:, cut:] + q1[p][0, :, pl.ds(cut, cut)].astype(F32)).astype(BF16)
        back1.append((one, go(s1[p].at[2], q1[p].at[2], nb(d, -1))))

    def out_rows(part):
        return inc_ref.at[pl.ds(part * sub, sub), :]

    x_end(va1, va2, mig_a, out_rows(0), out_rows(1))
    y_end(zb1, zb2, mig_b, out_rows(2), out_rows(3))

    for p in range(3):
        a1, a2, a3 = place(p)
        back1[p][0].wait_recv()
        back1[p][1].wait_recv()
        fin[:, pl.ds(starts[p], sizes[p])] = (
            t1[p][a1] + q1[p][1].astype(F32) + q1[p][2].astype(F32)
        )
    last = go(fin.at[pl.ds(pl.multiple_of(8 * oc, 8), 8), :], finr, sibling)
    routed_ref[:, mine] = fin[pl.ds(pl.multiple_of(8 * c, 8), 8), :].astype(BF16)
    last.wait_recv()
    routed_ref[:, other] = finr[...].astype(BF16)
    done_sending()


def body(hidden_in, routes, gates, gate_proj, up_proj, down_proj, query, kv_cache, lengths, moving, pair_mask):
    tokens, width = hidden_in.shape
    half = width // 2
    sizes = part_sizes(half)
    ff = gate_proj.shape[2]
    requests, slots, kvw = kv_cache.shape
    heads = query.shape[1]
    sub = slots // 4

    def per_part(*lead, dtype=BF16, extra=False):
        return [
            pltpu.VMEM((*lead, s + (GATE_TILE if extra and p == GATE_PART else 0)), dtype)
            for p, s in enumerate(sizes)
        ]

    mig = (
        [pltpu.VMEM((2, sub, kvw), BF16)] * 8
    )
    scratch = [
        *per_part(4, 4, 4, 16, extra=True),
        pltpu.VMEM((4, half, ff), BF16),
        pltpu.VMEM((2, ff, half), BF16),
        pltpu.VMEM((4, 4, 4, 4, 16, ff), F32),
        pltpu.VMEM((2, 4, 4, 4, 16, ff), F32),
        pltpu.VMEM((2, 4, 4, 4, 16, ff), BF16),
        pltpu.VMEM((2, 4, 4, 4, 16, GATE_TILE), F32),
        pltpu.VMEM((4, 64, max(sizes)), F32),
        *per_part(4, 4, 16),
        *per_part(4, 4, 16),
        *per_part(4, 4, 16),
        *per_part(4, 64, dtype=F32),
        *per_part(3, 64),
        *per_part(3, 64),
        *per_part(4, 16, dtype=F32),
        *per_part(3, 16),
        *per_part(3, 16),
        pltpu.VMEM((8, half + GATE_TILE), BF16),
        pltpu.VMEM((8, half + GATE_TILE), BF16),
        pltpu.VMEM((16, half), F32),
        pltpu.VMEM((8, half), F32),
        pltpu.VMEM((requests, slots, kvw), BF16),
        pltpu.VMEM((requests, heads, kvw), BF16),
        *mig,
        *mig,
        pltpu.SemaphoreType.DMA((160,)),
        pltpu.SemaphoreType.DMA((160,)),
        pltpu.SemaphoreType.DMA((8,)),
    ]
    vmem = pl.BlockSpec(memory_space=pltpu.VMEM)
    smem = pl.BlockSpec(memory_space=pltpu.SMEM)
    anywhere = pl.BlockSpec(memory_space=pl.ANY)
    routed, attention, incoming = pl.pallas_call(
        kernel,
        out_shape=(
            jax.ShapeDtypeStruct((tokens, width), BF16),
            jax.ShapeDtypeStruct((requests, heads, LAT), BF16),
            jax.ShapeDtypeStruct((slots, kvw), BF16),
        ),
        in_specs=[vmem, vmem, vmem, anywhere, anywhere, anywhere, anywhere, anywhere, smem, smem, smem],
        out_specs=(vmem, vmem, vmem),
        scratch_shapes=scratch,
        compiler_params=pltpu.CompilerParams(
            collective_id=0, has_side_effects=True, vmem_limit_bytes=64 * 1024 * 1024
        ),
        cost_estimate=pl.CostEstimate(flops=13_000_000_000, bytes_accessed=20_000_000, transcendentals=800_000),
    )(
        hidden_in, routes, gates, gate_proj[0], up_proj[0], down_proj[0], query, kv_cache, lengths, moving, pair_mask
    )
    return routed, attention, incoming[None]


def solution(mesh):
    return jax.shard_map(
        body,
        mesh=mesh,
        in_specs=(
            P(("rank", "expert"), None),
            P(("rank", "expert"), None),
            P(("rank", "expert"), None),
            P("expert", None, "rank"),
            P("expert", None, "rank"),
            P("expert", "rank", None),
            P(("rank", "expert"), None, None),
            P(("rank", "expert"), None, None),
            P(("rank", "expert")),
            P(("rank", "expert")),
            P(),
        ),
        out_specs=(
            P(("rank", "expert"), None),
            P(("rank", "expert"), None, None),
            P(("rank", "expert"), None, None),
        ),
        check_vma=False,
    )
```

```python
import functools

import jax
import jax.numpy as jnp
from jax import lax
from jax.experimental import pallas as pl
from jax.experimental.pallas import tpu as pltpu
from jax.sharding import PartitionSpec as P

LAT = 512
SCALE = 192.0 ** (-0.5)
MESH = pl.DeviceIdType.MESH
F32 = jnp.float32
BF16 = jnp.bfloat16
GATE_TILE = 128

DIMS = ((1, 0, 2), (2, 1, 0), (0, 2, 1))
GATE_PART = 2


def part_sizes(half):
    if half == 3584:
        return (1792, 896, 896)
    return (half // 3,) * 3


def kernel(
    hid_ref, routes_ref, gates_ref, wg_ref, wu_ref, wd_ref, q_ref, kv_ref, len_ref, mov_ref, mask_ref,
    routed_ref, att_ref, inc_ref,
    x0, x1, x2, w, dn, acc, rb, h, gbuf, tmp,
    f3_0, f3_1, f3_2, r3p_0, r3p_1, r3p_2, r3m_0, r3m_1, r3m_2, t2_0, t2_1, t2_2,
    s2_0, s2_1, s2_2, q2_0, q2_1, q2_2, s1_0, s1_1, s1_2, q1_0, q1_1, q1_2,
    stage_s, stage_r, fin, finr, kvv, qv,
    ya1, ya2, za1, za2, va1, va2, ua, sa, yb1, yb2, zb1, zb2, vb1, vb2, ub, sb,
    send_sems, recv_sems, local_sems,
):
    half = hid_ref.shape[1] // 2
    sizes = part_sizes(half)
    starts = (0, sizes[0], sizes[0] + sizes[1])
    xs, f3, r3p, r3m = (x0, x1, x2), (f3_0, f3_1, f3_2), (r3p_0, r3p_1, r3p_2), (r3m_0, r3m_1, r3m_2)
    t2, s2, q2 = (t2_0, t2_1, t2_2), (s2_0, s2_1, s2_2), (q2_0, q2_1, q2_2)
    s1, q1 = (s1_0, s1_1, s1_2), (q1_0, q1_1, q1_2)
    ff = wg_ref.shape[1]

    r = lax.axis_index("rank")
    e = lax.axis_index("expert")
    c = e % 2
    oc = 1 - c
    y = r % 4
    z = e // 4
    x = (r // 4) * 2 + (e // 2) % 2
    pos = (x, y, z)

    def at_chip(px, py, pz, core):
        return ((px // 2) * 4 + py, pz * 4 + (px % 2) * 2 + core)

    def nb(dim, delta):
        moved = [(v + delta + 4) % 4 if i == dim else v for i, v in enumerate(pos)]
        return at_chip(*moved, c)

    sibling = at_chip(x, y, z, oc)
    y_one = at_chip(x, y + 1 - 2 * (y % 2), z, c)
    y_three = at_chip(x, 3 - y, z, c)

    counter = [0]
    started = []

    def rc(src, dst, device):
        i = counter[0]
        counter[0] += 1
        return pltpu.make_async_remote_copy(
            src_ref=src, dst_ref=dst, send_sem=send_sems.at[i], recv_sem=recv_sems.at[i],
            device_id=device, device_id_type=MESH,
        )

    def go(src, dst, device):
        d = rc(src, dst, device)
        d.start()
        started.append(d)
        return d

    def done_sending():
        for d in started:
            d.wait_send()
        started.clear()

    locals_ = []

    def lc(src, dst):
        d = pltpu.make_async_copy(src, dst, local_sems.at[len(locals_)])
        locals_.append(d)
        d.start()
        return d

    lkv = lc(kv_ref, kvv)
    lq = lc(q_ref, qv)
    mine = pl.ds(pl.multiple_of(c * half, 128), half)
    other = pl.ds(pl.multiple_of(oc * half, 128), half)

    lane = lax.broadcasted_iota(jnp.int32, (8, GATE_TILE), 1)
    gate_rows = jnp.zeros((8, GATE_TILE), F32)
    wide_gates = gates_ref[...].astype(F32)
    names = routes_ref[...]
    for k in range(routes_ref.shape[1]):
        gate_rows = gate_rows + jnp.where(lane == names[:, k : k + 1], wide_gates[:, k : k + 1], 0.0)
    stage_s[:, pl.ds(0, half)] = hid_ref[:, other]
    stage_s[:, pl.ds(half, GATE_TILE)] = gate_rows.astype(BF16)

    barrier = pltpu.get_barrier_semaphore()
    for device in (nb(0, 1), nb(0, -1), nb(1, 1), nb(1, -1), nb(2, 1), nb(2, -1), sibling):
        pl.semaphore_signal(barrier, inc=1, device_id=device, device_id_type=MESH)
    pl.semaphore_wait(barrier, 7)

    tok = go(stage_s, stage_r, sibling)
    tok.wait_recv()
    cf = c.astype(F32)
    own_wide = jnp.concatenate([hid_ref[:, mine].astype(F32), gate_rows], axis=1)
    got_wide = stage_r[...].astype(F32)
    top = own_wide * (1.0 - cf) + got_wide * cf
    bottom = got_wide * (1.0 - cf) + own_wide * cf
    block = jnp.concatenate([top, bottom], axis=0).astype(BF16)

    def place(p):
        return tuple(pos[d] for d in DIMS[p])

    def near(v, delta):
        return (v + delta + 4) % 4

    for p in range(3):
        a1, a2, a3 = place(p)
        end = half + GATE_TILE if p == GATE_PART else starts[p] + sizes[p]
        xs[p][a3, a2, a1] = block[:, starts[p] : end]

    offs = (0, -1, 1, 2)

    def both_ways(ref, dim):
        return go(ref, ref, nb(dim, 1)), go(ref, ref, nb(dim, -1))

    g1, g2, g3 = [], [[None] * 4 for _ in range(3)], [[None] * 4 for _ in range(3)]
    own3 = [[None] * 4 for _ in range(3)]

    def block_at(p, k):
        a1, a2, a3 = place(p)
        return xs[p].at[a3, a2, near(a1, offs[k])]

    def second(p, k):
        g2[p][k] = both_ways(block_at(p, k), DIMS[p][1])

    def third_own(p, k):
        own3[p][k] = both_ways(block_at(p, k), DIMS[p][2])

    def third_line(p, k):
        a1, a2, a3 = place(p)
        g3[p][k] = both_ways(xs[p].at[a3, near(a2, offs[k])], DIMS[p][2])

    def side_of(k):
        return 1 if k % 2 == 0 else -1

    for p in range(3):
        g1.append(both_ways(block_at(p, 0), DIMS[p][0]))
    for p in range(3):
        second(p, 0)
    for p in range(3):
        third_own(p, 0)

    gate_cols = pl.ds(pl.multiple_of(2 * c * ff, 128), ff)
    up_cols = pl.ds(pl.multiple_of((2 * c + 1) * ff, 128), ff)
    lwg = lc(wg_ref.at[mine, :], w.at[:, gate_cols])
    lwu = lc(wu_ref.at[mine, :], w.at[:, up_cols])
    lwd = lc(wd_ref.at[:, mine], dn.at[c])
    rwg = go(wg_ref.at[other, :], w.at[:, gate_cols], sibling)
    rwu = go(wu_ref.at[other, :], w.at[:, up_cols], sibling)
    rwd = go(wd_ref.at[:, other], dn.at[c], sibling)

    mask = mask_ref[0]
    m_y = mask % 4
    m_x = mask // 4
    sub = ya1.shape[1]
    step_rows = 48 if sub % 48 == 0 else 16

    def for_rows(fn):
        @pl.loop(0, sub // step_rows)
        def _(i):
            fn(pl.ds(pl.multiple_of(i * step_rows, 16), step_rows))

    def pick_rows(dst, dst_slot, part):
        which = mov_ref[0]
        limit = len_ref[which]

        def one(rows):
            first = part * sub + rows.start
            piece = kvv[which, pl.ds(pl.multiple_of(first, 16), step_rows), :].astype(F32)
            at = lax.broadcasted_iota(jnp.int32, piece.shape, 1)
            dst[dst_slot, rows, :] = jnp.where(at < limit, piece, 0.0).astype(BF16)

        for_rows(one)

    def move_rows(dst, src, src_slot):
        def one(rows):
            dst[rows, :] = src[src_slot, rows, :]

        for_rows(one)

    def y_first(b1, b2):
        return go(b1.at[0], b1.at[1], y_one), go(b2.at[0], b2.at[1], y_three)

    def y_second(b1, b2, z1, z2, stage, first):
        first[0].wait_recv()
        first[1].wait_recv()
        move_rows(stage.at[0], b1, jnp.where(m_y == 3, 0, 1))
        s3 = go(stage.at[0], z1.at[1], y_three)
        move_rows(stage.at[1], b2, jnp.where(m_y == 1, 0, 1))
        s1_ = go(stage.at[1], z2.at[1], y_one)
        move_rows(z1.at[0], b1, jnp.where(m_y == 1, 1, 0))
        move_rows(z2.at[0], b2, jnp.where(m_y == 3, 1, 0))
        return s3, s1_

    def y_end(z1, z2, second, dst1, dst2):
        second[0].wait_recv()
        second[1].wait_recv()
        move_rows(dst1, z1, jnp.where(m_y <= 1, 0, 1))
        move_rows(dst2, z2, jnp.where((m_y == 0) | (m_y == 3), 0, 1))

    def x_first(v1, v2, u):
        return go(v1.at[0], u.at[0], nb(0, 1)), go(v2.at[0], u.at[1], nb(0, -1))

    def x_second(v1, v2, u, first):
        first[0].wait_recv()
        a = go(u.at[0], v1.at[1], nb(0, 1))
        first[1].wait_recv()
        return a, go(u.at[1], v2.at[1], nb(0, -1))

    def x_end(v1, v2, second, dst1, dst2):
        second[0].wait_recv()
        second[1].wait_recv()
        move_rows(dst1, v1, m_x)
        move_rows(dst2, v2, m_x)

    g1f = []
    for p in range(3):
        a1, a2, a3 = place(p)
        cut = xs[p].shape[4] // 256 * 128
        rest = xs[p].shape[4] - cut
        g1[p][0].wait_recv()
        left = xs[p].at[a3, a2, near(a1, -1), :, pl.ds(0, cut)]
        one = go(left, left, nb(DIMS[p][0], 1))
        g1[p][1].wait_recv()
        right = xs[p].at[a3, a2, near(a1, 1), :, pl.ds(cut, rest)]
        g1f.append((one, go(right, right, nb(DIMS[p][0], -1))))
    for p in range(3):
        second(p, 1)
        second(p, 2)
    for p in range(3):
        third_own(p, 1)
        third_own(p, 2)

    lq.wait()
    lkv.wait()

    def attend(b):
        kv = kvv[b]
        scores = lax.dot_general(qv[b], kv, (((0,), (0,)), ((), ())), preferred_element_type=F32) * SCALE
        valid = lax.broadcasted_iota(jnp.int32, scores.shape, 1) < len_ref[b]
        scores = jnp.where(valid, scores, -1e30)
        top_score = jnp.max(scores, axis=-1, keepdims=True)
        weights = jnp.where(valid, jnp.exp(scores - top_score), 0.0)
        total = jnp.sum(weights, axis=-1, keepdims=True)
        mixed = lax.dot_general(
            weights.astype(BF16), kv[:LAT, :], (((1,), (1,)), ((), ())), preferred_element_type=F32
        )
        att_ref[b] = (mixed / total).astype(BF16)

    g2f, own3f, g3f = ([[None] * 4 for _ in range(3)] for _ in range(3))

    def arrived(pair, k):
        pair[0 if k % 2 == 0 else 1].wait_recv()

    def rest_arrived(pair, k):
        pair[1 if k % 2 == 0 else 0].wait_recv()

    def second_on(p, k):
        a1, a2, a3 = place(p)
        arrived(g2[p][k], k)
        ref = xs[p].at[a3, near(a2, -side_of(k)), near(a1, offs[k])]
        g2f[p][k] = go(ref, ref, nb(DIMS[p][1], side_of(k)))

    def own_on(p, k):
        a1, a2, a3 = place(p)
        arrived(own3[p][k], k)
        ref = xs[p].at[near(a3, -side_of(k)), a2, near(a1, offs[k])]
        own3f[p][k] = go(ref, ref, nb(DIMS[p][2], side_of(k)))

    def line_on(p, k):
        a1, a2, a3 = place(p)
        arrived(g3[p][k], k)
        ref = xs[p].at[near(a3, -side_of(k)), near(a2, offs[k])]
        g3f[p][k] = (go(ref, ref, nb(DIMS[p][2], side_of(k))),)

    for p in range(3):
        second_on(p, 0)
    for p in range(3):
        own_on(p, 0)
    for p in range(3):
        g1f[p][0].wait_recv()
        g1f[p][1].wait_recv()
        second(p, 3)
    for p in range(3):
        third_own(p, 3)

    attend(0)

    for p in range(3):
        second_on(p, 1)
        second_on(p, 2)
    for p in range(3):
        own_on(p, 1)
        own_on(p, 2)

    @pl.loop(0, 4)
    def _(i):
        for j in range(4):
            acc[i, j] = jnp.zeros(acc.shape[2:], F32)

    for p in range(3):
        second_on(p, 3)
        for k in range(4):
            rest_arrived(g2[p][k], k)
        third_line(p, 1)
        third_line(p, 2)
    for p in range(3):
        own_on(p, 3)

    attend(1)

    for p in range(3):
        for k in range(4):
            g2f[p][k].wait_recv()
        third_line(p, 3)

    pick_rows(ya1, 0, 0)
    pick_rows(ya2, 0, 1)
    mig_a = y_first(ya1, ya2)
    pick_rows(vb1, 0, 2)
    pick_rows(vb2, 0, 3)
    mig_b = x_first(vb1, vb2, ub)

    def rows_of(p, j):
        full = slice(None)
        if p == 0:
            return [(i, full, j) for i in range(4)]
        if p == 1:
            return [(j, i, full) for i in range(4)]
        return [(full, j, i) for i in range(4)]

    lwg.wait()
    lwu.wait()
    rwg.wait_recv()
    rwu.wait_recv()

    def index_of(p, i3, i2):
        full = slice(None)
        return ((i2, full, i3), (i3, i2, full), (full, i3, i2))[p]

    def project(p, lines):
        lhs = jnp.concatenate(
            [xs[p][i3, i2, :, :, : sizes[p]].reshape(64, sizes[p]) for i3, i2 in lines], axis=0
        )

        res = jnp.dot(lhs, w[pl.ds(starts[p], sizes[p]), :], preferred_element_type=F32)
        for i, line in enumerate(lines):
            at = index_of(p, *line)
            acc[at] = acc[at] + res[64 * i : 64 * i + 64].reshape(4, 16, 4 * ff)

    def lines_at(p, delta, which):
        a1, a2, a3 = place(p)
        return [(near(a3, delta), near(a2, offs[k])) for k in which]

    for p in range(3):
        line_on(p, 1)
        line_on(p, 2)
    for p in range(3):
        project(p, lines_at(p, 0, range(4)))
    attend(2)
    for p in range(3):
        a1, a2, a3 = place(p)
        g3[p][3][0].wait_recv()
        left = xs[p].at[near(a3, -1), near(a2, 2), pl.ds(0, 2)]
        one = go(left, left, nb(DIMS[p][2], 1))
        g3[p][3][1].wait_recv()
        right = xs[p].at[near(a3, 1), near(a2, 2), pl.ds(2, 2)]
        g3f[p][3] = (one, go(right, right, nb(DIMS[p][2], -1)))
    mig_a = y_second(ya1, ya2, za1, za2, sa, mig_a)
    mig_b = x_second(vb1, vb2, ub, mig_b)
    for p in range(3):
        for k in range(4):
            rest_arrived(own3[p][k], k)
        rest_arrived(g3[p][1], 1)
        rest_arrived(g3[p][2], 2)
        project(p, lines_at(p, -1, range(4)) + lines_at(p, 1, range(4)))
    attend(3)
    for p in (1, 2, 0):
        for k in range(4):
            own3f[p][k].wait_recv()
        for k in (1, 2):
            g3f[p][k][0].wait_recv()
        project(p, lines_at(p, 2, range(3)))
    lwd.wait()
    rwd.wait_recv()
    for p in (1, 2, 0):
        for d in g3f[p][3]:
            d.wait_recv()
        project(p, lines_at(p, 2, (3,)))

    part_sends = []
    for k in (3, 1, 2, 0):
        xx = near(x, offs[k])
        part_sends.append(
            go(acc.at[xx, :, :, :, pl.ds(pl.multiple_of(2 * oc * ff, 128), 2 * ff)], rb.at[xx], sibling)
        )

    for n in range(2):
        pick = lax.broadcasted_iota(jnp.int32, (GATE_TILE, GATE_TILE), 0) == e - c + n
        pick = jnp.where(pick, 1.0, 0.0).astype(BF16)
        for j in range(4):
            table = xs[GATE_PART][j][:, :, :, sizes[GATE_PART] :].reshape(256, GATE_TILE)
            spread = jnp.dot(table, pick, preferred_element_type=F32).reshape(4, 4, 16, GATE_TILE)
            for i, index in enumerate(rows_of(GATE_PART, j)):
                gbuf[(n, *index)] = spread[i]

    hid_sends = []
    for at, k in enumerate((3, 1, 2, 0)):
        xx = near(x, offs[k])
        part_sends[at].wait_recv()
        gate = acc[xx, :, :, :, gate_cols] + rb[xx, :, :, :, :ff]
        up = acc[xx, :, :, :, up_cols] + rb[xx, :, :, :, ff:]
        h[c, xx] = (gate * (1.0 / (1.0 + jnp.exp(-gate))) * up).astype(BF16)
        hid_sends.append(go(h.at[c, xx], h.at[c, xx], sibling))
    done_sending()

    def down(p, j, dst):
        def pull(ref, n):
            return jnp.concatenate([ref[(n, *i)].reshape(64, ref.shape[-1]) for i in rows_of(p, j)], axis=0)

        hs = [pull(h, n) for n in range(2)]
        gs = [pull(gbuf, n) for n in range(2)]
        most = 896 if sizes[p] % 896 == 0 else 256
        gs = [jnp.concatenate([g] * (most // GATE_TILE), axis=1) for g in gs]

        def tile(first, width):
            cols = pl.ds(pl.multiple_of(starts[p] + first, 128), width)
            out = gs[0][:, :width] * jnp.dot(hs[0], dn[0, :, cols], preferred_element_type=F32)
            out = out + gs[1][:, :width] * jnp.dot(hs[1], dn[1, :, cols], preferred_element_type=F32)
            at = pl.ds(pl.multiple_of(first, 128), width)
            if dst.dtype == BF16:
                dst[:, :, :, at] = out.astype(BF16).reshape(4, 4, 16, width)
            else:
                dst[:, :, at] = out.reshape(4, 64, width)

        for first in range(0, sizes[p], most):
            tile(first, most)

    def cut_of(p):
        return sizes[p] // 256 * 128

    roffs = (2, -1, 1, 0)

    def down_to_tmp(p, j):
        view = tmp.at[:, :, pl.ds(0, sizes[p])]
        down(p, j, view)
        return view

    def put(p, which, k2, value):
        xs[p][which, k2, :, :, : sizes[p]] = value.astype(BF16).reshape(4, 16, sizes[p])

    def put_block(p, which, k2, i1, value):
        xs[p][which, k2, i1, :, : sizes[p]] = value.astype(BF16)

    def send3(p, which, k2, blocks, into, side):
        src = xs[p].at[which, k2, blocks, :, pl.ds(0, sizes[p])]
        return go(src, into[p].at[k2, blocks], nb(DIMS[p][2], side))

    fw3 = [[None] * 8 for _ in range(3)]
    hid_sends[0].wait_recv()
    for p in (1, 0, 2):
        a1, a2, a3 = place(p)
        if p == 0:
            for d in hid_sends[1:]:
                d.wait_recv()
        down(p, near(a3, 2), xs[p].at[0])

        def forward3(i2, blocks, into, side):
            src = xs[p].at[0, i2, blocks, :, pl.ds(0, sizes[p])]
            return go(src, f3[p].at[into, blocks], nb(DIMS[p][2], side))

        far = near(a2, 2)
        fw3[p][0] = (forward3(far, pl.ds(0, 2), 0, 1), forward3(far, pl.ds(2, 2), 0, -1))
        for k in (1, 2):
            fw3[p][k] = forward3(near(a2, roffs[k]), pl.ds(0, 4), k, side_of(k))
        for k in range(4):
            fw3[p][4 + k] = forward3(a2, near(a1, roffs[k]), 3, side_of(k))

    y_end(za1, za2, mig_a, va1.at[0], va2.at[0])
    mig_a = x_first(va1, va2, ua)
    x_end(vb1, vb2, mig_b, yb1.at[0], yb2.at[0])
    mig_b = y_first(yb1, yb2)

    to_side = {1: [[None] * 8 for _ in range(3)], -1: [[None] * 8 for _ in range(3)]}
    back3 = {1: r3p, -1: r3m}
    for p in (1, 2, 0):
        a1, a2, a3 = place(p)
        for side, which in ((1, 1), (-1, 2)):
            sent = to_side[side][p]
            view = down_to_tmp(p, near(a3, side))
            fw3[p][0][0 if side == 1 else 1].wait_recv()
            value = view[near(a2, 2)]
            first = 0 if side == 1 else 2
            added = f3[p][0, pl.ds(first, 2)].reshape(32, sizes[p]).astype(F32)
            if side == 1:
                value = jnp.concatenate([value[:32] + added, value[32:]], axis=0)
            else:
                value = jnp.concatenate([value[:32], value[32:] + added], axis=0)
            put(p, which, 0, value)
            sent[0] = send3(p, which, 0, pl.ds(0, 4), back3[side], side)
            for k in (1, 2):
                value = view[near(a2, roffs[k])]
                if side_of(k) == side:
                    fw3[p][k].wait_recv()
                    value = value + f3[p][k].reshape(64, sizes[p]).astype(F32)
                put(p, which, k, value)
                sent[k] = send3(p, which, k, pl.ds(0, 4), back3[side], side)
            for k in range(4):
                i1 = near(a1, roffs[k])
                value = view[a2, pl.ds(pl.multiple_of(i1 * 16, 16), 16), :]
                if side_of(k) == side:
                    fw3[p][4 + k].wait_recv()
                    value = value + f3[p][3, i1].astype(F32)
                put_block(p, which, 3, i1, value)
                sent[4 + k] = send3(p, which, 3, i1, back3[side], side)
    for p in (1, 2, 0):
        down(p, place(p)[2], t2[p])

    mig_a = x_second(va1, va2, ua, mig_a)
    mig_b = y_second(yb1, yb2, zb1, zb2, sb, mig_b)

    def settle(p, k):
        i2 = near(place(p)[1], roffs[k])
        to_side[1][p][k].wait_recv()
        to_side[-1][p][k].wait_recv()
        got = r3p[p][k].reshape(64, sizes[p]).astype(F32) + r3m[p][k].reshape(64, sizes[p]).astype(F32)
        t2[p][i2] = t2[p][i2] + got

    def t2_block(p, k, i1):
        return t2[p][near(place(p)[1], roffs[k]), pl.ds(pl.multiple_of(i1 * 16, 16), 16), :]

    def send2(p, which, i1, side):
        return go(s2[p].at[which, i1], q2[p].at[which, i1], nb(DIMS[p][1], side))

    fw2 = [[None] * 4 for _ in range(3)]
    for p in (1, 2, 0):
        settle(p, 0)
        for k in range(4):
            i1 = near(place(p)[0], roffs[k])
            s2[p][0, i1] = t2_block(p, 0, i1).astype(BF16)
            fw2[p][k] = send2(p, 0, i1, side_of(k))
    back2 = [[[None] * 4, [None] * 4] for _ in range(3)]
    for p in (1, 2, 0):
        settle(p, 1)
        settle(p, 2)
        for k in range(4):
            i1 = near(place(p)[0], roffs[k])
            fw2[p][k].wait_recv()
            for slot, side, line in ((1, 1, 2), (2, -1, 1)):
                value = t2_block(p, line, i1)
                if side_of(k) == side:
                    value = value + q2[p][0, i1].astype(F32)
                s2[p][slot, i1] = value.astype(BF16)
                back2[p][slot - 1][k] = send2(p, slot, i1, side)

    def settle_block(p, k):
        i1 = near(place(p)[0], roffs[k])
        to_side[1][p][4 + k].wait_recv()
        to_side[-1][p][4 + k].wait_recv()
        value = t2_block(p, 3, i1) + r3p[p][3, i1].astype(F32) + r3m[p][3, i1].astype(F32)
        back2[p][0][k].wait_recv()
        back2[p][1][k].wait_recv()
        return value + q2[p][1, i1].astype(F32) + q2[p][2, i1].astype(F32)

    fw1, back1 = [None] * 3, [[None, None] for _ in range(3)]
    for p in (1, 2, 0):
        d = DIMS[p][0]
        s1[p][0] = settle_block(p, 0).astype(BF16)
        cut = cut_of(p)
        left, right = pl.ds(0, cut), pl.ds(cut, sizes[p] - cut)
        fw1[p] = (
            go(s1[p].at[0, :, left], q1[p].at[0, :, left], nb(d, 1)),
            go(s1[p].at[0, :, right], q1[p].at[0, :, right], nb(d, -1)),
        )
    for p in (1, 2, 0):
        d = DIMS[p][0]
        cut = cut_of(p)
        value = settle_block(p, 1)
        fw1[p][1].wait_recv()
        s1[p][2, :, pl.ds(0, cut)] = value[:, :cut].astype(BF16)
        s1[p][2, :, pl.ds(cut, sizes[p] - cut)] = (value[:, cut:] + q1[p][0, :, pl.ds(cut, sizes[p] - cut)].astype(F32)).astype(BF16)
        back1[p][1] = go(s1[p].at[2], q1[p].at[2], nb(d, -1))
    for p in (1, 2, 0):
        d = DIMS[p][0]
        cut = cut_of(p)
        value = settle_block(p, 2)
        fw1[p][0].wait_recv()
        s1[p][1, :, pl.ds(0, cut)] = (value[:, :cut] + q1[p][0, :, pl.ds(0, cut)].astype(F32)).astype(BF16)
        s1[p][1, :, pl.ds(cut, sizes[p] - cut)] = value[:, cut:].astype(BF16)
        back1[p][0] = go(s1[p].at[1], q1[p].at[1], nb(d, 1))

    def out_rows(part):
        return inc_ref.at[pl.ds(part * sub, sub), :]

    x_end(va1, va2, mig_a, out_rows(0), out_rows(1))
    y_end(zb1, zb2, mig_b, out_rows(2), out_rows(3))

    for p in (1, 2, 0):
        back1[p][0].wait_recv()
        back1[p][1].wait_recv()
        fin[:, pl.ds(starts[p], sizes[p])] = (
            settle_block(p, 3) + q1[p][1].astype(F32) + q1[p][2].astype(F32)
        )
    last = go(fin.at[pl.ds(pl.multiple_of(8 * oc, 8), 8), :], finr, sibling)
    routed_ref[:, mine] = fin[pl.ds(pl.multiple_of(8 * c, 8), 8), :].astype(BF16)
    last.wait_recv()
    routed_ref[:, other] = finr[...].astype(BF16)
    done_sending()


def finish(a_ref, b_ref, c_ref, x_ref, y_ref, z_ref):
    x_ref[...] = a_ref[...]
    y_ref[...] = b_ref[...]
    z_ref[...] = c_ref[...]


def body(hidden_in, routes, gates, gate_proj, up_proj, down_proj, query, kv_cache, lengths, moving, pair_mask):
    tokens, width = hidden_in.shape
    half = width // 2
    sizes = part_sizes(half)
    ff = gate_proj.shape[2]
    kv_cache, query = jnp.swapaxes(kv_cache, 1, 2), jnp.swapaxes(query, 1, 2)
    requests, kvw, slots = kv_cache.shape
    heads = query.shape[2]
    sub = kvw // 4

    def per_part(*lead, dtype=BF16, extra=False):
        return [
            pltpu.VMEM((*lead, s + (GATE_TILE if extra and p == GATE_PART else 0)), dtype)
            for p, s in enumerate(sizes)
        ]

    mig = (
        [pltpu.VMEM((2, sub, slots), BF16)] * 8
    )
    scratch = [
        *per_part(4, 4, 4, 16, extra=True),
        pltpu.VMEM((half, 4 * ff), BF16),
        pltpu.VMEM((2, ff, half), BF16),
        pltpu.VMEM((4, 4, 4, 16, 4 * ff), F32),
        pltpu.VMEM((4, 4, 4, 16, 2 * ff), F32),
        pltpu.VMEM((2, 4, 4, 4, 16, ff), BF16),
        pltpu.VMEM((2, 4, 4, 4, 16, GATE_TILE), F32),
        pltpu.VMEM((4, 64, max(sizes)), F32),
        *per_part(4, 4, 16),
        *per_part(4, 4, 16),
        *per_part(4, 4, 16),
        *per_part(4, 64, dtype=F32),
        *per_part(3, 4, 16),
        *per_part(3, 4, 16),
        *per_part(3, 16),
        *per_part(3, 16),
        pltpu.VMEM((8, half + GATE_TILE), BF16),
        pltpu.VMEM((8, half + GATE_TILE), BF16),
        pltpu.VMEM((16, half), F32),
        pltpu.VMEM((8, half), F32),
        pltpu.VMEM((requests, kvw, slots), BF16),
        pltpu.VMEM((requests, kvw, heads), BF16),
        *mig,
        *mig,
        pltpu.SemaphoreType.DMA((272,)),
        pltpu.SemaphoreType.DMA((272,)),
        pltpu.SemaphoreType.DMA((8,)),
    ]
    vmem = pl.BlockSpec(memory_space=pltpu.VMEM)
    smem = pl.BlockSpec(memory_space=pltpu.SMEM)
    anywhere = pl.BlockSpec(memory_space=pl.ANY)
    routed, attention, incoming = pl.pallas_call(
        kernel,
        out_shape=(
            jax.ShapeDtypeStruct((tokens, width), BF16),
            jax.ShapeDtypeStruct((requests, heads, LAT), BF16),
            jax.ShapeDtypeStruct((kvw, slots), BF16),
        ),
        in_specs=[vmem, vmem, vmem, anywhere, anywhere, anywhere, anywhere, anywhere, smem, smem, smem],
        out_specs=(vmem, vmem, vmem),
        scratch_shapes=scratch,
        compiler_params=pltpu.CompilerParams(
            collective_id=0, has_side_effects=True, vmem_limit_bytes=64 * 1024 * 1024
        ),
        cost_estimate=pl.CostEstimate(flops=13_000_000_000, bytes_accessed=20_000_000, transcendentals=800_000),
    )(
        hidden_in, routes, gates, gate_proj[0], up_proj[0], down_proj[0], query, kv_cache, lengths, moving, pair_mask
    )
    results = (routed, attention, incoming)
    routed, attention, incoming = pl.pallas_call(
        finish,
        out_shape=tuple(jax.ShapeDtypeStruct(v.shape, v.dtype) for v in results),
        in_specs=[vmem] * 3,
        out_specs=(vmem,) * 3,
    )(*results)
    return routed, attention, incoming.T[None]


def solution(mesh):
    return jax.shard_map(
        body,
        mesh=mesh,
        in_specs=(
            P(("rank", "expert"), None),
            P(("rank", "expert"), None),
            P(("rank", "expert"), None),
            P("expert", None, "rank"),
            P("expert", None, "rank"),
            P("expert", "rank", None),
            P(("rank", "expert"), None, None),
            P(("rank", "expert"), None, None),
            P(("rank", "expert")),
            P(("rank", "expert")),
            P(),
        ),
        out_specs=(
            P(("rank", "expert"), None),
            P(("rank", "expert"), None, None),
            P(("rank", "expert"), None, None),
        ),
        check_vma=False,
    )
```

```python
import functools

import jax
import jax.numpy as jnp
from jax import lax
from jax.experimental import pallas as pl
from jax.experimental.pallas import tpu as pltpu
from jax.sharding import PartitionSpec as P

LAT = 512
SCALE = 192.0 ** (-0.5)
MESH = pl.DeviceIdType.MESH
F32 = jnp.float32
BF16 = jnp.bfloat16
GATE_TILE = 128

DIMS = ((1, 0, 2), (2, 1, 0), (0, 2, 1))
GATE_PART = 2


def part_sizes(half):
    if half == 3584:
        return (1536, 1024, 1024)
    return (half // 3,) * 3


def kernel(
    hid_ref, routes_ref, gates_ref, wg_ref, wu_ref, wd_ref, q_ref, kv_ref, len_ref, mov_ref, mask_ref,
    routed_ref, att_ref, inc_ref,
    x0, x1, x2, w, dn, acc, rb, h, gbuf, tmp0, tmp1, tmp2,
    f3_0, f3_1, f3_2, r3p_0, r3p_1, r3p_2, r3m_0, r3m_1, r3m_2, t2_0, t2_1, t2_2,
    s2_0, s2_1, s2_2, q2_0, q2_1, q2_2, s1_0, s1_1, s1_2, q1_0, q1_1, q1_2,
    stage_s, stage_r, fin, finr, kvv, qv,
    ya1, ya2, za1, za2, va1, va2, ua, sa, yb1, yb2, zb1, zb2, vb1, vb2, ub, sb,
    send_sems, recv_sems, local_sems,
):
    half = hid_ref.shape[1] // 2
    sizes = part_sizes(half)
    starts = (0, sizes[0], sizes[0] + sizes[1])
    xs, f3, r3p, r3m = (x0, x1, x2), (f3_0, f3_1, f3_2), (r3p_0, r3p_1, r3p_2), (r3m_0, r3m_1, r3m_2)
    tmp = (tmp0, tmp1, tmp2)
    t2, s2, q2 = (t2_0, t2_1, t2_2), (s2_0, s2_1, s2_2), (q2_0, q2_1, q2_2)
    s1, q1 = (s1_0, s1_1, s1_2), (q1_0, q1_1, q1_2)
    ff = wg_ref.shape[1]

    r = lax.axis_index("rank")
    e = lax.axis_index("expert")
    c = e % 2
    oc = 1 - c
    y = r % 4
    z = e // 4
    x = (r // 4) * 2 + (e // 2) % 2
    pos = (x, y, z)

    def at_chip(px, py, pz, core):
        return ((px // 2) * 4 + py, pz * 4 + (px % 2) * 2 + core)

    def nb(dim, delta):
        moved = [(v + delta + 4) % 4 if i == dim else v for i, v in enumerate(pos)]
        return at_chip(*moved, c)

    sibling = at_chip(x, y, z, oc)
    y_one = at_chip(x, y + 1 - 2 * (y % 2), z, c)
    y_three = at_chip(x, 3 - y, z, c)

    counter = [0]
    started = []

    def rc(src, dst, device):
        i = counter[0]
        counter[0] += 1
        return pltpu.make_async_remote_copy(
            src_ref=src, dst_ref=dst, send_sem=send_sems.at[i], recv_sem=recv_sems.at[i],
            device_id=device, device_id_type=MESH,
        )

    def go(src, dst, device):
        d = rc(src, dst, device)
        d.start()
        started.append(d)
        return d

    def done_sending():
        for d in started:
            d.wait_send()
        started.clear()

    locals_ = []

    def lc(src, dst):
        d = pltpu.make_async_copy(src, dst, local_sems.at[len(locals_)])
        locals_.append(d)
        d.start()
        return d

    lkv = lc(kv_ref, kvv)
    lq = lc(q_ref, qv)
    mine = pl.ds(pl.multiple_of(c * half, 128), half)
    other = pl.ds(pl.multiple_of(oc * half, 128), half)

    lane = lax.broadcasted_iota(jnp.int32, (8, GATE_TILE), 1)
    gate_rows = jnp.zeros((8, GATE_TILE), F32)
    wide_gates = gates_ref[...].astype(F32)
    names = routes_ref[...]
    for k in range(routes_ref.shape[1]):
        gate_rows = gate_rows + jnp.where(lane == names[:, k : k + 1], wide_gates[:, k : k + 1], 0.0)
    stage_s[:, pl.ds(0, half)] = hid_ref[:, other]
    stage_s[:, pl.ds(half, GATE_TILE)] = gate_rows.astype(BF16)

    barrier = pltpu.get_barrier_semaphore()
    for device in (nb(0, 1), nb(0, -1), nb(1, 1), nb(1, -1), nb(2, 1), nb(2, -1), sibling):
        pl.semaphore_signal(barrier, inc=1, device_id=device, device_id_type=MESH)
    pl.semaphore_wait(barrier, 7)

    tok = go(stage_s, stage_r, sibling)
    tok.wait_recv()
    cf = c.astype(F32)
    own_wide = jnp.concatenate([hid_ref[:, mine].astype(F32), gate_rows], axis=1)
    got_wide = stage_r[...].astype(F32)
    top = own_wide * (1.0 - cf) + got_wide * cf
    bottom = got_wide * (1.0 - cf) + own_wide * cf
    block = jnp.concatenate([top, bottom], axis=0).astype(BF16)

    def place(p):
        return tuple(pos[d] for d in DIMS[p])

    def near(v, delta):
        return (v + delta + 4) % 4

    for p in range(3):
        a1, a2, a3 = place(p)
        end = half + GATE_TILE if p == GATE_PART else starts[p] + sizes[p]
        xs[p][a3, a2, a1] = block[:, starts[p] : end]

    offs = (0, -1, 1, 2)

    def both_ways(ref, dim):
        return go(ref, ref, nb(dim, 1)), go(ref, ref, nb(dim, -1))

    g1, g2, g3 = [], [[None] * 4 for _ in range(3)], [[None] * 4 for _ in range(3)]
    own3 = [[None] * 4 for _ in range(3)]

    def block_at(p, k):
        a1, a2, a3 = place(p)
        return xs[p].at[a3, a2, near(a1, offs[k])]

    def second(p, k):
        g2[p][k] = both_ways(block_at(p, k), DIMS[p][1])

    def third_own(p, k):
        own3[p][k] = both_ways(block_at(p, k), DIMS[p][2])

    def third_line(p, k):
        a1, a2, a3 = place(p)
        g3[p][k] = both_ways(xs[p].at[a3, near(a2, offs[k])], DIMS[p][2])

    def side_of(k):
        return 1 if k % 2 == 0 else -1

    for p in range(3):
        g1.append(both_ways(block_at(p, 0), DIMS[p][0]))
    for p in range(3):
        second(p, 0)
    for p in range(3):
        third_own(p, 0)

    gate_cols = pl.ds(pl.multiple_of(2 * c * ff, 128), ff)
    up_cols = pl.ds(pl.multiple_of((2 * c + 1) * ff, 128), ff)
    lwg = lc(wg_ref.at[mine, :], w.at[:, gate_cols])
    lwu = lc(wu_ref.at[mine, :], w.at[:, up_cols])
    lwd = lc(wd_ref.at[:, mine], dn.at[c])
    rwg = go(wg_ref.at[other, :], w.at[:, gate_cols], sibling)
    rwu = go(wu_ref.at[other, :], w.at[:, up_cols], sibling)
    rwd = go(wd_ref.at[:, other], dn.at[c], sibling)

    mask = mask_ref[0]
    m_y = mask % 4
    m_x = mask // 4
    sub = ya1.shape[1]
    step_rows = 48 if sub % 48 == 0 else 16

    def for_rows(fn):
        @pl.loop(0, sub // step_rows)
        def _(i):
            fn(pl.ds(pl.multiple_of(i * step_rows, 16), step_rows))

    def pick_rows(dst, dst_slot, part):
        which = mov_ref[0]
        limit = len_ref[which]

        def one(rows):
            first = part * sub + rows.start
            piece = kvv[which, pl.ds(pl.multiple_of(first, 16), step_rows), :].astype(F32)
            at = lax.broadcasted_iota(jnp.int32, piece.shape, 1)
            dst[dst_slot, rows, :] = jnp.where(at < limit, piece, 0.0).astype(BF16)

        for_rows(one)

    def move_rows(dst, src, src_slot):
        def one(rows):
            dst[rows, :] = src[src_slot, rows, :]

        for_rows(one)

    def y_first(b1, b2):
        return go(b1.at[0], b1.at[1], y_one), go(b2.at[0], b2.at[1], y_three)

    def y_second(b1, b2, z1, z2, stage, first):
        first[0].wait_recv()
        first[1].wait_recv()
        move_rows(stage.at[0], b1, jnp.where(m_y == 3, 0, 1))
        s3 = go(stage.at[0], z1.at[1], y_three)
        move_rows(stage.at[1], b2, jnp.where(m_y == 1, 0, 1))
        s1_ = go(stage.at[1], z2.at[1], y_one)
        move_rows(z1.at[0], b1, jnp.where(m_y == 1, 1, 0))
        move_rows(z2.at[0], b2, jnp.where(m_y == 3, 1, 0))
        return s3, s1_

    def y_end(z1, z2, second, dst1, dst2):
        second[0].wait_recv()
        second[1].wait_recv()
        move_rows(dst1, z1, jnp.where(m_y <= 1, 0, 1))
        move_rows(dst2, z2, jnp.where((m_y == 0) | (m_y == 3), 0, 1))

    def x_first(v1, v2, u):
        return go(v1.at[0], u.at[0], nb(0, 1)), go(v2.at[0], u.at[1], nb(0, -1))

    def x_second(v1, v2, u, first):
        first[0].wait_recv()
        a = go(u.at[0], v1.at[1], nb(0, 1))
        first[1].wait_recv()
        return a, go(u.at[1], v2.at[1], nb(0, -1))

    def x_end(v1, v2, second, dst1, dst2):
        second[0].wait_recv()
        second[1].wait_recv()
        move_rows(dst1, v1, m_x)
        move_rows(dst2, v2, m_x)

    g1f = []
    for p in range(3):
        a1, a2, a3 = place(p)
        cut = xs[p].shape[4] // 256 * 128
        rest = xs[p].shape[4] - cut
        g1[p][0].wait_recv()
        left = xs[p].at[a3, a2, near(a1, -1), :, pl.ds(0, cut)]
        one = go(left, left, nb(DIMS[p][0], 1))
        g1[p][1].wait_recv()
        right = xs[p].at[a3, a2, near(a1, 1), :, pl.ds(cut, rest)]
        g1f.append((one, go(right, right, nb(DIMS[p][0], -1))))
    for p in range(3):
        second(p, 1)
        second(p, 2)
    for p in range(3):
        third_own(p, 1)
        third_own(p, 2)

    lq.wait()
    lkv.wait()

    def attend(b):
        kv = kvv[b]
        scores = lax.dot_general(qv[b], kv, (((0,), (0,)), ((), ())), preferred_element_type=F32) * SCALE
        valid = lax.broadcasted_iota(jnp.int32, scores.shape, 1) < len_ref[b]
        scores = jnp.where(valid, scores, -1e30)
        top_score = jnp.max(scores, axis=-1, keepdims=True)
        weights = jnp.where(valid, jnp.exp(scores - top_score), 0.0)
        total = jnp.sum(weights, axis=-1, keepdims=True)
        mixed = lax.dot_general(
            weights.astype(BF16), kv[:LAT, :], (((1,), (1,)), ((), ())), preferred_element_type=F32
        )
        att_ref[b] = (mixed / total).astype(BF16)

    g2f, own3f, g3f = ([[None] * 4 for _ in range(3)] for _ in range(3))

    def arrived(pair, k):
        pair[0 if k % 2 == 0 else 1].wait_recv()

    def rest_arrived(pair, k):
        pair[1 if k % 2 == 0 else 0].wait_recv()

    def second_on(p, k):
        a1, a2, a3 = place(p)
        arrived(g2[p][k], k)
        ref = xs[p].at[a3, near(a2, -side_of(k)), near(a1, offs[k])]
        g2f[p][k] = go(ref, ref, nb(DIMS[p][1], side_of(k)))

    def own_on(p, k):
        a1, a2, a3 = place(p)
        arrived(own3[p][k], k)
        ref = xs[p].at[near(a3, -side_of(k)), a2, near(a1, offs[k])]
        own3f[p][k] = go(ref, ref, nb(DIMS[p][2], side_of(k)))

    def line_on(p, k):
        a1, a2, a3 = place(p)
        arrived(g3[p][k], k)
        ref = xs[p].at[near(a3, -side_of(k)), near(a2, offs[k])]
        g3f[p][k] = (go(ref, ref, nb(DIMS[p][2], side_of(k))),)

    for p in range(3):
        second_on(p, 0)
    for p in range(3):
        own_on(p, 0)
    for p in range(3):
        g1f[p][0].wait_recv()
        g1f[p][1].wait_recv()
        second(p, 3)
    for p in range(3):
        third_own(p, 3)

    attend(0)

    for p in range(3):
        second_on(p, 1)
        second_on(p, 2)
    for p in range(3):
        own_on(p, 1)
        own_on(p, 2)

    @pl.loop(0, 4)
    def _(i):
        for j in range(4):
            acc[i, j] = jnp.zeros(acc.shape[2:], F32)

    for p in range(3):
        second_on(p, 3)
        for k in range(4):
            rest_arrived(g2[p][k], k)
        third_line(p, 1)
        third_line(p, 2)
    for p in range(3):
        own_on(p, 3)

    attend(1)

    for p in range(3):
        for k in range(4):
            g2f[p][k].wait_recv()
        third_line(p, 3)

    pick_rows(ya1, 0, 0)
    pick_rows(ya2, 0, 1)
    mig_a = y_first(ya1, ya2)
    pick_rows(vb1, 0, 2)
    pick_rows(vb2, 0, 3)
    mig_b = x_first(vb1, vb2, ub)

    def rows_of(p, j):
        full = slice(None)
        if p == 0:
            return [(i, full, j) for i in range(4)]
        if p == 1:
            return [(j, i, full) for i in range(4)]
        return [(full, j, i) for i in range(4)]

    lwg.wait()
    lwu.wait()
    rwg.wait_recv()
    rwu.wait_recv()

    def index_of(p, i3, i2):
        full = slice(None)
        return ((i2, full, i3), (i3, i2, full), (full, i3, i2))[p]

    def project(p, lines):
        lhs = jnp.concatenate(
            [xs[p][i3, i2, :, :, : sizes[p]].reshape(64, sizes[p]) for i3, i2 in lines], axis=0
        )

        res = jnp.dot(lhs, w[pl.ds(starts[p], sizes[p]), :], preferred_element_type=F32)
        for i, line in enumerate(lines):
            at = index_of(p, *line)
            acc[at] = acc[at] + res[64 * i : 64 * i + 64].reshape(4, 16, 4 * ff)

    def lines_at(p, delta, which):
        a1, a2, a3 = place(p)
        return [(near(a3, delta), near(a2, offs[k])) for k in which]

    for p in range(3):
        line_on(p, 1)
        line_on(p, 2)
    for p in range(3):
        project(p, lines_at(p, 0, range(4)))
    attend(2)
    for p in range(3):
        for k in range(4):
            rest_arrived(own3[p][k], k)
        rest_arrived(g3[p][1], 1)
        rest_arrived(g3[p][2], 2)
        project(p, lines_at(p, -1, range(3)) + lines_at(p, 1, range(3)))
    attend(3)
    for p in range(3):
        a1, a2, a3 = place(p)
        g3[p][3][0].wait_recv()
        left = xs[p].at[near(a3, -1), near(a2, 2), pl.ds(0, 2)]
        one = go(left, left, nb(DIMS[p][2], 1))
        g3[p][3][1].wait_recv()
        right = xs[p].at[near(a3, 1), near(a2, 2), pl.ds(2, 2)]
        g3f[p][3] = (one, go(right, right, nb(DIMS[p][2], -1)))
    mig_a = y_second(ya1, ya2, za1, za2, sa, mig_a)
    mig_b = x_second(vb1, vb2, ub, mig_b)
    for p in (1, 2, 0):
        for k in range(4):
            own3f[p][k].wait_recv()
        for k in (1, 2):
            g3f[p][k][0].wait_recv()
        project(p, lines_at(p, 2, range(3)) + lines_at(p, -1, (3,)) + lines_at(p, 1, (3,)))
    lwd.wait()
    rwd.wait_recv()
    for p in (1, 2, 0):
        for d in g3f[p][3]:
            d.wait_recv()
        project(p, lines_at(p, 2, (3,)))

    part_sends = []
    for k in (3, 1, 2, 0):
        xx = near(x, offs[k])
        part_sends.append(
            go(acc.at[xx, :, :, :, pl.ds(pl.multiple_of(2 * oc * ff, 128), 2 * ff)], rb.at[xx], sibling)
        )

    y_end(za1, za2, mig_a, va1.at[0], va2.at[0])
    mig_a = x_first(va1, va2, ua)
    x_end(vb1, vb2, mig_b, yb1.at[0], yb2.at[0])
    mig_b = y_first(yb1, yb2)

    for n in range(2):
        pick = lax.broadcasted_iota(jnp.int32, (GATE_TILE, GATE_TILE), 0) == e - c + n
        pick = jnp.where(pick, 1.0, 0.0).astype(BF16)
        for j in range(4):
            table = xs[GATE_PART][j][:, :, :, sizes[GATE_PART] :].reshape(256, GATE_TILE)
            spread = jnp.dot(table, pick, preferred_element_type=F32).reshape(4, 4, 16, GATE_TILE)
            for i, index in enumerate(rows_of(GATE_PART, j)):
                gbuf[(n, *index)] = spread[i]

    hid_sends = []
    for at, k in enumerate((3, 1, 2, 0)):
        xx = near(x, offs[k])
        part_sends[at].wait_recv()
        gate = acc[xx, :, :, :, gate_cols] + rb[xx, :, :, :, :ff]
        up = acc[xx, :, :, :, up_cols] + rb[xx, :, :, :, ff:]
        h[c, xx] = (gate * (1.0 / (1.0 + jnp.exp(-gate))) * up).astype(BF16)
        hid_sends.append(go(h.at[c, xx], h.at[c, xx], sibling))
    done_sending()

    def down(p, j, dst):
        def pull(ref, n):
            return jnp.concatenate([ref[(n, *i)].reshape(64, ref.shape[-1]) for i in rows_of(p, j)], axis=0)

        hs = [pull(h, n) for n in range(2)]
        gs = [pull(gbuf, n) for n in range(2)]
        most = sizes[p] if sizes[p] <= 1152 else sizes[p] // 2
        gs = [jnp.concatenate([g] * (most // GATE_TILE), axis=1) for g in gs]

        def tile(first, width):
            cols = pl.ds(pl.multiple_of(starts[p] + first, 128), width)
            out = gs[0][:, :width] * jnp.dot(hs[0], dn[0, :, cols], preferred_element_type=F32)
            out = out + gs[1][:, :width] * jnp.dot(hs[1], dn[1, :, cols], preferred_element_type=F32)
            at = pl.ds(pl.multiple_of(first, 128), width)
            if dst.dtype == BF16:
                dst[:, :, :, at] = out.astype(BF16).reshape(4, 4, 16, width)
            else:
                dst[:, :, at] = out.reshape(4, 64, width)

        for first in range(0, sizes[p], most):
            tile(first, most)

    def cut_of(p):
        return sizes[p] // 256 * 128

    roffs = (2, -1, 1, 0)

    def put(p, which, k2, value):
        xs[p][which, k2, :, :, : sizes[p]] = value.astype(BF16).reshape(4, 16, sizes[p])

    def put_block(p, which, k2, i1, value):
        xs[p][which, k2, i1, :, : sizes[p]] = value.astype(BF16)

    def send3(p, which, k2, blocks, into, side):
        src = xs[p].at[which, k2, blocks, :, pl.ds(0, sizes[p])]
        return go(src, into[p].at[k2, blocks], nb(DIMS[p][2], side))

    fw3 = [[None] * 8 for _ in range(3)]
    hid_sends[0].wait_recv()
    for p in (1, 0, 2):
        a1, a2, a3 = place(p)
        if p == 0:
            for d in hid_sends[1:]:
                d.wait_recv()
        down(p, near(a3, 2), xs[p].at[0])

        def forward3(i2, blocks, into, side):
            src = xs[p].at[0, i2, blocks, :, pl.ds(0, sizes[p])]
            return go(src, f3[p].at[into, blocks], nb(DIMS[p][2], side))

        far = near(a2, 2)
        fw3[p][0] = (forward3(far, pl.ds(0, 2), 0, 1), forward3(far, pl.ds(2, 2), 0, -1))
        for k in (1, 2):
            fw3[p][k] = forward3(near(a2, roffs[k]), pl.ds(0, 4), k, side_of(k))
        for k in range(4):
            fw3[p][4 + k] = forward3(a2, near(a1, roffs[k]), 3, side_of(k))

    to_side = {1: [[None] * 8 for _ in range(3)], -1: [[None] * 8 for _ in range(3)]}
    back3 = {1: r3p, -1: r3m}
    sides = ((1, 1, 2), (-1, 2, 1))

    def line_to(p, side, which, k, added):
        value = tmp[p][which - 1, near(place(p)[1], roffs[k])]
        if added:
            fw3[p][k].wait_recv()
            value = value + f3[p][k].reshape(64, sizes[p]).astype(F32)
        put(p, which, k, value)
        to_side[side][p][k] = send3(p, which, k, pl.ds(0, 4), back3[side], side)

    for p in (1, 2, 0):
        for side, which, joined in sides:
            down(p, near(place(p)[2], side), tmp[p].at[which - 1])
            line_to(p, side, which, 3 - joined, False)
    for p in (1, 2, 0):
        for side, which, joined in sides:
            fw3[p][0][which - 1].wait_recv()
            value = tmp[p][which - 1, near(place(p)[1], 2)]
            added = f3[p][0, pl.ds(2 * which - 2, 2)].reshape(32, sizes[p]).astype(F32)
            if side == 1:
                value = jnp.concatenate([value[:32] + added, value[32:]], axis=0)
            else:
                value = jnp.concatenate([value[:32], value[32:] + added], axis=0)
            put(p, which, 0, value)
            to_side[side][p][0] = send3(p, which, 0, pl.ds(0, 4), back3[side], side)
    mig_a = x_second(va1, va2, ua, mig_a)
    mig_b = y_second(yb1, yb2, zb1, zb2, sb, mig_b)
    for p in (1, 2, 0):
        for side, which, joined in sides:
            line_to(p, side, which, joined, True)
    for p in (1, 2, 0):
        a1, a2, a3 = place(p)
        for k in range(4):
            i1 = near(a1, roffs[k])
            for side, which, joined in sides:
                value = tmp[p][which - 1, a2, pl.ds(pl.multiple_of(i1 * 16, 16), 16), :]
                if side_of(k) == side:
                    fw3[p][4 + k].wait_recv()
                    value = value + f3[p][3, i1].astype(F32)
                put_block(p, which, 3, i1, value)
                to_side[side][p][4 + k] = send3(p, which, 3, i1, back3[side], side)
    for p in (1, 2, 0):
        down(p, place(p)[2], t2[p])

    def settle(p, k):
        i2 = near(place(p)[1], roffs[k])
        to_side[1][p][k].wait_recv()
        to_side[-1][p][k].wait_recv()
        got = r3p[p][k].reshape(64, sizes[p]).astype(F32) + r3m[p][k].reshape(64, sizes[p]).astype(F32)
        t2[p][i2] = t2[p][i2] + got

    def t2_block(p, k, i1):
        return t2[p][near(place(p)[1], roffs[k]), pl.ds(pl.multiple_of(i1 * 16, 16), 16), :]

    def send2(p, which, i1, side):
        return go(s2[p].at[which, i1], q2[p].at[which, i1], nb(DIMS[p][1], side))

    fw2 = [[None] * 4 for _ in range(3)]
    for p in (1, 2, 0):
        settle(p, 0)
        for k in range(4):
            i1 = near(place(p)[0], roffs[k])
            s2[p][0, i1] = t2_block(p, 0, i1).astype(BF16)
            fw2[p][k] = send2(p, 0, i1, side_of(k))
    back2 = [[[None] * 4, [None] * 4] for _ in range(3)]
    for p in (1, 2, 0):
        settle(p, 1)
        settle(p, 2)
        for k in range(4):
            i1 = near(place(p)[0], roffs[k])
            fw2[p][k].wait_recv()
            for slot, side, line in ((1, 1, 2), (2, -1, 1)):
                value = t2_block(p, line, i1)
                if side_of(k) == side:
                    value = value + q2[p][0, i1].astype(F32)
                s2[p][slot, i1] = value.astype(BF16)
                back2[p][slot - 1][k] = send2(p, slot, i1, side)

    def settle_block(p, k):
        i1 = near(place(p)[0], roffs[k])
        to_side[1][p][4 + k].wait_recv()
        to_side[-1][p][4 + k].wait_recv()
        value = t2_block(p, 3, i1) + r3p[p][3, i1].astype(F32) + r3m[p][3, i1].astype(F32)
        back2[p][0][k].wait_recv()
        back2[p][1][k].wait_recv()
        return value + q2[p][1, i1].astype(F32) + q2[p][2, i1].astype(F32)

    fw1, back1 = [None] * 3, [[None, None] for _ in range(3)]
    for p in (1, 2, 0):
        d = DIMS[p][0]
        s1[p][0] = settle_block(p, 0).astype(BF16)
        cut = cut_of(p)
        left, right = pl.ds(0, cut), pl.ds(cut, sizes[p] - cut)
        fw1[p] = (
            go(s1[p].at[0, :, left], q1[p].at[0, :, left], nb(d, 1)),
            go(s1[p].at[0, :, right], q1[p].at[0, :, right], nb(d, -1)),
        )
    for p in (1, 2, 0):
        d = DIMS[p][0]
        cut = cut_of(p)
        value = settle_block(p, 1)
        fw1[p][1].wait_recv()
        s1[p][2, :, pl.ds(0, cut)] = value[:, :cut].astype(BF16)
        s1[p][2, :, pl.ds(cut, sizes[p] - cut)] = (value[:, cut:] + q1[p][0, :, pl.ds(cut, sizes[p] - cut)].astype(F32)).astype(BF16)
        back1[p][1] = go(s1[p].at[2], q1[p].at[2], nb(d, -1))
    for p in (1, 2, 0):
        d = DIMS[p][0]
        cut = cut_of(p)
        value = settle_block(p, 2)
        fw1[p][0].wait_recv()
        s1[p][1, :, pl.ds(0, cut)] = (value[:, :cut] + q1[p][0, :, pl.ds(0, cut)].astype(F32)).astype(BF16)
        s1[p][1, :, pl.ds(cut, sizes[p] - cut)] = value[:, cut:].astype(BF16)
        back1[p][0] = go(s1[p].at[1], q1[p].at[1], nb(d, 1))

    def out_rows(part):
        return inc_ref.at[pl.ds(part * sub, sub), :]

    x_end(va1, va2, mig_a, out_rows(0), out_rows(1))
    y_end(zb1, zb2, mig_b, out_rows(2), out_rows(3))

    for p in (1, 2, 0):
        back1[p][0].wait_recv()
        back1[p][1].wait_recv()
        fin[:, pl.ds(starts[p], sizes[p])] = (
            settle_block(p, 3) + q1[p][1].astype(F32) + q1[p][2].astype(F32)
        )
    last = go(fin.at[pl.ds(pl.multiple_of(8 * oc, 8), 8), :], finr, sibling)
    routed_ref[:, mine] = fin[pl.ds(pl.multiple_of(8 * c, 8), 8), :].astype(BF16)
    last.wait_recv()
    routed_ref[:, other] = finr[...].astype(BF16)
    done_sending()


def finish(a_ref, b_ref, c_ref, x_ref, y_ref, z_ref):
    x_ref[...] = a_ref[...]
    y_ref[...] = b_ref[...]
    z_ref[...] = c_ref[...]


def body(hidden_in, routes, gates, gate_proj, up_proj, down_proj, query, kv_cache, lengths, moving, pair_mask):
    tokens, width = hidden_in.shape
    half = width // 2
    sizes = part_sizes(half)
    ff = gate_proj.shape[2]
    kv_cache, query = jnp.swapaxes(kv_cache, 1, 2), jnp.swapaxes(query, 1, 2)
    requests, kvw, slots = kv_cache.shape
    heads = query.shape[2]
    sub = kvw // 4

    def per_part(*lead, dtype=BF16, extra=False):
        return [
            pltpu.VMEM((*lead, s + (GATE_TILE if extra and p == GATE_PART else 0)), dtype)
            for p, s in enumerate(sizes)
        ]

    mig = (
        [pltpu.VMEM((2, sub, slots), BF16)] * 8
    )
    scratch = [
        *per_part(4, 4, 4, 16, extra=True),
        pltpu.VMEM((half, 4 * ff), BF16),
        pltpu.VMEM((2, ff, half), BF16),
        pltpu.VMEM((4, 4, 4, 16, 4 * ff), F32),
        pltpu.VMEM((4, 4, 4, 16, 2 * ff), F32),
        pltpu.VMEM((2, 4, 4, 4, 16, ff), BF16),
        pltpu.VMEM((2, 4, 4, 4, 16, GATE_TILE), F32),
        *per_part(2, 4, 64, dtype=F32),
        *per_part(4, 4, 16),
        *per_part(4, 4, 16),
        *per_part(4, 4, 16),
        *per_part(4, 64, dtype=F32),
        *per_part(3, 4, 16),
        *per_part(3, 4, 16),
        *per_part(3, 16),
        *per_part(3, 16),
        pltpu.VMEM((8, half + GATE_TILE), BF16),
        pltpu.VMEM((8, half + GATE_TILE), BF16),
        pltpu.VMEM((16, half), F32),
        pltpu.VMEM((8, half), F32),
        pltpu.VMEM((requests, kvw, slots), BF16),
        pltpu.VMEM((requests, kvw, heads), BF16),
        *mig,
        *mig,
        pltpu.SemaphoreType.DMA((272,)),
        pltpu.SemaphoreType.DMA((272,)),
        pltpu.SemaphoreType.DMA((8,)),
    ]
    vmem = pl.BlockSpec(memory_space=pltpu.VMEM)
    smem = pl.BlockSpec(memory_space=pltpu.SMEM)
    anywhere = pl.BlockSpec(memory_space=pl.ANY)
    routed, attention, incoming = pl.pallas_call(
        kernel,
        out_shape=(
            jax.ShapeDtypeStruct((tokens, width), BF16),
            jax.ShapeDtypeStruct((requests, heads, LAT), BF16),
            jax.ShapeDtypeStruct((kvw, slots), BF16),
        ),
        in_specs=[vmem, vmem, vmem, anywhere, anywhere, anywhere, anywhere, anywhere, smem, smem, smem],
        out_specs=(vmem, vmem, vmem),
        scratch_shapes=scratch,
        compiler_params=pltpu.CompilerParams(
            collective_id=0, has_side_effects=True, vmem_limit_bytes=64 * 1024 * 1024
        ),
        cost_estimate=pl.CostEstimate(flops=13_000_000_000, bytes_accessed=20_000_000, transcendentals=800_000),
    )(
        hidden_in, routes, gates, gate_proj[0], up_proj[0], down_proj[0], query, kv_cache, lengths, moving, pair_mask
    )
    results = (routed, attention, incoming)
    routed, attention, incoming = pl.pallas_call(
        finish,
        out_shape=tuple(jax.ShapeDtypeStruct(v.shape, v.dtype) for v in results),
        in_specs=[vmem] * 3,
        out_specs=(vmem,) * 3,
    )(*results)
    return routed, attention, incoming.T[None]


def solution(mesh):
    return jax.shard_map(
        body,
        mesh=mesh,
        in_specs=(
            P(("rank", "expert"), None),
            P(("rank", "expert"), None),
            P(("rank", "expert"), None),
            P("expert", None, "rank"),
            P("expert", None, "rank"),
            P("expert", "rank", None),
            P(("rank", "expert"), None, None),
            P(("rank", "expert"), None, None),
            P(("rank", "expert")),
            P(("rank", "expert")),
            P(),
        ),
        out_specs=(
            P(("rank", "expert"), None),
            P(("rank", "expert"), None, None),
            P(("rank", "expert"), None, None),
        ),
        check_vma=False,
    )
```

```python
import functools

import jax
import jax.numpy as jnp
from jax import lax
from jax.experimental import pallas as pl
from jax.experimental.pallas import tpu as pltpu
from jax.sharding import PartitionSpec as P

LAT = 512
SCALE = 192.0 ** (-0.5)
MESH = pl.DeviceIdType.MESH
F32 = jnp.float32
BF16 = jnp.bfloat16
GATE_TILE = 128

DIMS = ((1, 0, 2), (2, 1, 0), (0, 2, 1))
GATE_PART = 2


def part_sizes(half):
    if half == 3584:
        return (1536, 1024, 1024)
    return (half // 3,) * 3


def kernel(
    hid_ref, routes_ref, gates_ref, wg_ref, wu_ref, wd_ref, q_ref, kv_ref, len_ref, mov_ref, mask_ref,
    routed_ref, att_ref, inc_ref,
    x0, x1, x2, w, dn, acc, rb, h, gbuf, tmp0, tmp1, tmp2,
    f3_0, f3_1, f3_2, r3p_0, r3p_1, r3p_2, r3m_0, r3m_1, r3m_2, t2_0, t2_1, t2_2,
    s2_0, s2_1, s2_2, q2_0, q2_1, q2_2, s1_0, s1_1, s1_2, q1_0, q1_1, q1_2,
    stage_s, stage_r, fin, finr, kvv, qv,
    ya1, ya2, za1, za2, va1, va2, ua, sa, yb1, yb2, zb1, zb2, vb1, vb2, ub, sb,
    send_sems, recv_sems, local_sems,
):
    half = hid_ref.shape[1] // 2
    sizes = part_sizes(half)
    starts = (0, sizes[0], sizes[0] + sizes[1])
    xs, f3, r3p, r3m = (x0, x1, x2), (f3_0, f3_1, f3_2), (r3p_0, r3p_1, r3p_2), (r3m_0, r3m_1, r3m_2)
    tmp = (tmp0, tmp1, tmp2)
    t2, s2, q2 = (t2_0, t2_1, t2_2), (s2_0, s2_1, s2_2), (q2_0, q2_1, q2_2)
    s1, q1 = (s1_0, s1_1, s1_2), (q1_0, q1_1, q1_2)
    ff = wg_ref.shape[1]

    r = lax.axis_index("rank")
    e = lax.axis_index("expert")
    c = e % 2
    oc = 1 - c
    y = r % 4
    z = e // 4
    x = (r // 4) * 2 + (e // 2) % 2
    pos = (x, y, z)

    def at_chip(px, py, pz, core):
        return ((px // 2) * 4 + py, pz * 4 + (px % 2) * 2 + core)

    def nb(dim, delta):
        moved = [(v + delta + 4) % 4 if i == dim else v for i, v in enumerate(pos)]
        return at_chip(*moved, c)

    sibling = at_chip(x, y, z, oc)
    y_one = at_chip(x, y + 1 - 2 * (y % 2), z, c)
    y_three = at_chip(x, 3 - y, z, c)

    counter = [0]
    started = []

    def rc(src, dst, device):
        i = counter[0]
        counter[0] += 1
        return pltpu.make_async_remote_copy(
            src_ref=src, dst_ref=dst, send_sem=send_sems.at[i], recv_sem=recv_sems.at[i],
            device_id=device, device_id_type=MESH,
        )

    def go(src, dst, device):
        d = rc(src, dst, device)
        d.start()
        started.append(d)
        return d

    def done_sending():
        for d in started:
            d.wait_send()
        started.clear()

    locals_ = []

    def lc(src, dst):
        d = pltpu.make_async_copy(src, dst, local_sems.at[len(locals_)])
        locals_.append(d)
        d.start()
        return d

    lkv = lc(kv_ref, kvv)
    lq = lc(q_ref, qv)
    mine = pl.ds(pl.multiple_of(c * half, 128), half)
    other = pl.ds(pl.multiple_of(oc * half, 128), half)

    lane = lax.broadcasted_iota(jnp.int32, (8, GATE_TILE), 1)
    gate_rows = jnp.zeros((8, GATE_TILE), F32)
    wide_gates = gates_ref[...].astype(F32)
    names = routes_ref[...]
    for k in range(routes_ref.shape[1]):
        gate_rows = gate_rows + jnp.where(lane == names[:, k : k + 1], wide_gates[:, k : k + 1], 0.0)
    stage_s[:, pl.ds(0, half)] = hid_ref[:, other]
    stage_s[:, pl.ds(half, GATE_TILE)] = gate_rows.astype(BF16)

    barrier = pltpu.get_barrier_semaphore()
    for device in [nb(dim, delta) for dim in range(3) for delta in (1, -1, 2)] + [sibling]:
        pl.semaphore_signal(barrier, inc=1, device_id=device, device_id_type=MESH)
    pl.semaphore_wait(barrier, 10)

    tok = go(stage_s, stage_r, sibling)
    tok.wait_recv()
    cf = c.astype(F32)
    own_wide = jnp.concatenate([hid_ref[:, mine].astype(F32), gate_rows], axis=1)
    got_wide = stage_r[...].astype(F32)
    top = own_wide * (1.0 - cf) + got_wide * cf
    bottom = got_wide * (1.0 - cf) + own_wide * cf
    block = jnp.concatenate([top, bottom], axis=0).astype(BF16)

    def place(p):
        return tuple(pos[d] for d in DIMS[p])

    def near(v, delta):
        return (v + delta + 4) % 4

    for p in range(3):
        a1, a2, a3 = place(p)
        end = half + GATE_TILE if p == GATE_PART else starts[p] + sizes[p]
        xs[p][a3, a2, a1] = block[:, starts[p] : end]

    offs = (0, -1, 1, 2)

    def both_ways(ref, dim):
        return go(ref, ref, nb(dim, 1)), go(ref, ref, nb(dim, -1))

    g1, g2, g3 = [], [[None] * 4 for _ in range(3)], [[None] * 4 for _ in range(3)]
    own3 = [[None] * 4 for _ in range(3)]

    def block_at(p, k):
        a1, a2, a3 = place(p)
        return xs[p].at[a3, a2, near(a1, offs[k])]

    def second(p, k):
        g2[p][k] = both_ways(block_at(p, k), DIMS[p][1])

    def third_own(p, k):
        own3[p][k] = both_ways(block_at(p, k), DIMS[p][2])

    def third_line(p, k):
        a1, a2, a3 = place(p)
        g3[p][k] = both_ways(xs[p].at[a3, near(a2, offs[k])], DIMS[p][2])

    def side_of(k):
        return 1 if k % 2 == 0 else -1

    for p in range(3):
        g1.append(both_ways(block_at(p, 0), DIMS[p][0]))
    for p in range(3):
        second(p, 0)
    for p in range(3):
        third_own(p, 0)

    gate_cols = pl.ds(pl.multiple_of(2 * c * ff, 128), ff)
    up_cols = pl.ds(pl.multiple_of((2 * c + 1) * ff, 128), ff)
    lwg = lc(wg_ref.at[mine, :], w.at[:, gate_cols])
    lwu = lc(wu_ref.at[mine, :], w.at[:, up_cols])
    lwd = lc(wd_ref.at[:, mine], dn.at[c])
    rwg = go(wg_ref.at[other, :], w.at[:, gate_cols], sibling)
    rwu = go(wu_ref.at[other, :], w.at[:, up_cols], sibling)
    rwd = go(wd_ref.at[:, other], dn.at[c], sibling)

    mask = mask_ref[0]
    m_y = mask % 4
    m_x = mask // 4
    sub = ya1.shape[1]
    step_rows = 48 if sub % 48 == 0 else 16

    def for_rows(fn):
        @pl.loop(0, sub // step_rows)
        def _(i):
            fn(pl.ds(pl.multiple_of(i * step_rows, 16), step_rows))

    def pick_rows(dst, dst_slot, part):
        which = mov_ref[0]
        limit = len_ref[which]

        def one(rows):
            first = part * sub + rows.start
            piece = kvv[which, pl.ds(pl.multiple_of(first, 16), step_rows), :].astype(F32)
            at = lax.broadcasted_iota(jnp.int32, piece.shape, 1)
            dst[dst_slot, rows, :] = jnp.where(at < limit, piece, 0.0).astype(BF16)

        for_rows(one)

    def move_rows(dst, src, src_slot):
        def one(rows):
            dst[rows, :] = src[src_slot, rows, :]

        for_rows(one)

    def y_first(b1, b2):
        return go(b1.at[0], b1.at[1], y_one), go(b2.at[0], b2.at[1], y_three)

    def y_second(b1, b2, z1, z2, stage, first):
        first[0].wait_recv()
        first[1].wait_recv()
        move_rows(stage.at[0], b1, jnp.where(m_y == 3, 0, 1))
        s3 = go(stage.at[0], z1.at[1], y_three)
        move_rows(stage.at[1], b2, jnp.where(m_y == 1, 0, 1))
        s1_ = go(stage.at[1], z2.at[1], y_one)
        move_rows(z1.at[0], b1, jnp.where(m_y == 1, 1, 0))
        move_rows(z2.at[0], b2, jnp.where(m_y == 3, 1, 0))
        return s3, s1_

    def y_end(z1, z2, second, dst1, dst2):
        second[0].wait_recv()
        second[1].wait_recv()
        move_rows(dst1, z1, jnp.where(m_y <= 1, 0, 1))
        move_rows(dst2, z2, jnp.where((m_y == 0) | (m_y == 3), 0, 1))

    def x_first(v1, v2, u):
        return go(v1.at[0], u.at[0], nb(0, 1)), go(v2.at[0], u.at[1], nb(0, -1))

    def x_second(v1, v2, u, first):
        first[0].wait_recv()
        a = go(u.at[0], v1.at[1], nb(0, 1))
        first[1].wait_recv()
        return a, go(u.at[1], v2.at[1], nb(0, -1))

    def x_end(v1, v2, second, dst1, dst2):
        second[0].wait_recv()
        second[1].wait_recv()
        move_rows(dst1, v1, m_x)
        move_rows(dst2, v2, m_x)

    g1f = []
    for p in range(3):
        a1, a2, a3 = place(p)
        cut = xs[p].shape[4] // 256 * 128
        rest = xs[p].shape[4] - cut
        g1[p][0].wait_recv()
        left = xs[p].at[a3, a2, near(a1, -1), :, pl.ds(0, cut)]
        one = go(left, left, nb(DIMS[p][0], 1))
        g1[p][1].wait_recv()
        right = xs[p].at[a3, a2, near(a1, 1), :, pl.ds(cut, rest)]
        g1f.append((one, go(right, right, nb(DIMS[p][0], -1))))
    for p in range(3):
        second(p, 1)
        second(p, 2)
    for p in range(3):
        third_own(p, 1)
        third_own(p, 2)

    lq.wait()
    lkv.wait()

    def attend(b):
        kv = kvv[b]
        scores = lax.dot_general(qv[b], kv, (((0,), (0,)), ((), ())), preferred_element_type=F32) * SCALE
        valid = lax.broadcasted_iota(jnp.int32, scores.shape, 1) < len_ref[b]
        scores = jnp.where(valid, scores, -1e30)
        top_score = jnp.max(scores, axis=-1, keepdims=True)
        weights = jnp.where(valid, jnp.exp(scores - top_score), 0.0)
        total = jnp.sum(weights, axis=-1, keepdims=True)
        mixed = lax.dot_general(
            weights.astype(BF16), kv[:LAT, :], (((1,), (1,)), ((), ())), preferred_element_type=F32
        )
        att_ref[b] = (mixed / total).astype(BF16)

    g2f, own3f, g3f = ([[None] * 4 for _ in range(3)] for _ in range(3))

    def arrived(pair, k):
        pair[0 if k % 2 == 0 else 1].wait_recv()

    def rest_arrived(pair, k):
        pair[1 if k % 2 == 0 else 0].wait_recv()

    def second_on(p, k):
        a1, a2, a3 = place(p)
        arrived(g2[p][k], k)
        ref = xs[p].at[a3, near(a2, -side_of(k)), near(a1, offs[k])]
        g2f[p][k] = go(ref, ref, nb(DIMS[p][1], side_of(k)))

    def own_on(p, k):
        a1, a2, a3 = place(p)
        arrived(own3[p][k], k)
        ref = xs[p].at[near(a3, -side_of(k)), a2, near(a1, offs[k])]
        own3f[p][k] = go(ref, ref, nb(DIMS[p][2], side_of(k)))

    def line_on(p, k):
        a1, a2, a3 = place(p)
        arrived(g3[p][k], k)
        ref = xs[p].at[near(a3, -side_of(k)), near(a2, offs[k])]
        g3f[p][k] = (go(ref, ref, nb(DIMS[p][2], side_of(k))),)

    for p in range(3):
        second_on(p, 0)
    for p in range(3):
        own_on(p, 0)
    for p in range(3):
        g1f[p][0].wait_recv()
        g1f[p][1].wait_recv()
        second(p, 3)
    for p in range(3):
        third_own(p, 3)

    attend(0)

    for p in range(3):
        second_on(p, 1)
        second_on(p, 2)
    for p in range(3):
        own_on(p, 1)
        own_on(p, 2)

    @pl.loop(0, 4)
    def _(i):
        for j in range(4):
            acc[i, j] = jnp.zeros(acc.shape[2:], F32)

    for p in range(3):
        second_on(p, 3)
        for k in range(4):
            rest_arrived(g2[p][k], k)
        third_line(p, 1)
        third_line(p, 2)
    for p in range(3):
        own_on(p, 3)

    attend(1)

    for p in range(3):
        for k in range(4):
            g2f[p][k].wait_recv()
        third_line(p, 3)

    pick_rows(ya1, 0, 0)
    pick_rows(ya2, 0, 1)
    mig_a = y_first(ya1, ya2)
    pick_rows(vb1, 0, 2)
    pick_rows(vb2, 0, 3)
    mig_b = x_first(vb1, vb2, ub)

    def rows_of(p, j):
        full = slice(None)
        if p == 0:
            return [(i, full, j) for i in range(4)]
        if p == 1:
            return [(j, i, full) for i in range(4)]
        return [(full, j, i) for i in range(4)]

    lwg.wait()
    lwu.wait()
    rwg.wait_recv()
    rwu.wait_recv()

    def index_of(p, i3, i2):
        full = slice(None)
        return ((i2, full, i3), (i3, i2, full), (full, i3, i2))[p]

    def project(p, lines):
        lhs = jnp.concatenate(
            [xs[p][i3, i2, :, :, : sizes[p]].reshape(64, sizes[p]) for i3, i2 in lines], axis=0
        )

        res = jnp.dot(lhs, w[pl.ds(starts[p], sizes[p]), :], preferred_element_type=F32)
        for i, line in enumerate(lines):
            at = index_of(p, *line)
            acc[at] = acc[at] + res[64 * i : 64 * i + 64].reshape(4, 16, 4 * ff)

    def lines_at(p, delta, which):
        a1, a2, a3 = place(p)
        return [(near(a3, delta), near(a2, offs[k])) for k in which]

    for p in range(3):
        line_on(p, 1)
        line_on(p, 2)
    for p in range(3):
        project(p, lines_at(p, 0, range(4)))
    attend(2)
    for p in range(3):
        for k in range(4):
            rest_arrived(own3[p][k], k)
        rest_arrived(g3[p][1], 1)
        rest_arrived(g3[p][2], 2)
        project(p, lines_at(p, -1, range(3)) + lines_at(p, 1, range(3)))
    attend(3)
    for p in range(3):
        a1, a2, a3 = place(p)
        g3[p][3][0].wait_recv()
        left = xs[p].at[near(a3, -1), near(a2, 2), pl.ds(0, 2)]
        one = go(left, left, nb(DIMS[p][2], 1))
        g3[p][3][1].wait_recv()
        right = xs[p].at[near(a3, 1), near(a2, 2), pl.ds(2, 2)]
        g3f[p][3] = (one, go(right, right, nb(DIMS[p][2], -1)))
    mig_a = y_second(ya1, ya2, za1, za2, sa, mig_a)
    mig_b = x_second(vb1, vb2, ub, mig_b)
    for p in (1, 2, 0):
        for k in range(4):
            own3f[p][k].wait_recv()
        for k in (1, 2):
            g3f[p][k][0].wait_recv()
        project(p, lines_at(p, 2, range(3)) + lines_at(p, -1, (3,)) + lines_at(p, 1, (3,)))
    lwd.wait()
    rwd.wait_recv()
    for p in (1, 2, 0):
        for d in g3f[p][3]:
            d.wait_recv()
        project(p, lines_at(p, 2, (3,)))

    part_sends = []
    for k in (3, 1, 2, 0):
        xx = near(x, offs[k])
        part_sends.append(
            go(acc.at[xx, :, :, :, pl.ds(pl.multiple_of(2 * oc * ff, 128), 2 * ff)], rb.at[xx], sibling)
        )

    y_end(za1, za2, mig_a, va1.at[0], va2.at[0])
    mig_a = x_first(va1, va2, ua)
    x_end(vb1, vb2, mig_b, yb1.at[0], yb2.at[0])
    mig_b = y_first(yb1, yb2)

    for n in range(2):
        pick = lax.broadcasted_iota(jnp.int32, (GATE_TILE, GATE_TILE), 0) == e - c + n
        pick = jnp.where(pick, 1.0, 0.0).astype(BF16)
        for j in range(4):
            table = xs[GATE_PART][j][:, :, :, sizes[GATE_PART] :].reshape(256, GATE_TILE)
            spread = jnp.dot(table, pick, preferred_element_type=F32).reshape(4, 4, 16, GATE_TILE)
            for i, index in enumerate(rows_of(GATE_PART, j)):
                gbuf[(n, *index)] = spread[i]

    hid_sends = []
    for at, k in enumerate((3, 1, 2, 0)):
        xx = near(x, offs[k])
        part_sends[at].wait_recv()
        gate = acc[xx, :, :, :, gate_cols] + rb[xx, :, :, :, :ff]
        up = acc[xx, :, :, :, up_cols] + rb[xx, :, :, :, ff:]
        h[c, xx] = (gate * (1.0 / (1.0 + jnp.exp(-gate))) * up).astype(BF16)
        hid_sends.append(go(h.at[c, xx], h.at[c, xx], sibling))
    done_sending()

    def down(p, j, dst):
        def pull(ref, n):
            return jnp.concatenate([ref[(n, *i)].reshape(64, ref.shape[-1]) for i in rows_of(p, j)], axis=0)

        hs = [pull(h, n) for n in range(2)]
        gs = [pull(gbuf, n) for n in range(2)]
        most = sizes[p] if sizes[p] <= 1152 else sizes[p] // 2
        gs = [jnp.concatenate([g] * (most // GATE_TILE), axis=1) for g in gs]

        def tile(first, width):
            cols = pl.ds(pl.multiple_of(starts[p] + first, 128), width)
            out = gs[0][:, :width] * jnp.dot(hs[0], dn[0, :, cols], preferred_element_type=F32)
            out = out + gs[1][:, :width] * jnp.dot(hs[1], dn[1, :, cols], preferred_element_type=F32)
            at = pl.ds(pl.multiple_of(first, 128), width)
            if dst.dtype == BF16:
                dst[:, :, :, at] = out.astype(BF16).reshape(4, 4, 16, width)
            else:
                dst[:, :, at] = out.reshape(4, 64, width)

        for first in range(0, sizes[p], most):
            tile(first, most)

    roffs = (2, -1, 1, 0)

    def put(p, which, k2, value):
        xs[p][which, k2, :, :, : sizes[p]] = value.astype(BF16).reshape(4, 16, sizes[p])

    def put_block(p, which, k2, i1, value):
        xs[p][which, k2, i1, :, : sizes[p]] = value.astype(BF16)

    def send3(p, which, k2, blocks, into, side):
        src = xs[p].at[which, k2, blocks, :, pl.ds(0, sizes[p])]
        return go(src, into[p].at[k2, blocks], nb(DIMS[p][2], side))

    fw3 = [[None] * 8 for _ in range(3)]
    hid_sends[0].wait_recv()
    for p in (1, 0, 2):
        a1, a2, a3 = place(p)
        if p == 0:
            for d in hid_sends[1:]:
                d.wait_recv()
        down(p, near(a3, 2), xs[p].at[0])

        def forward3(i2, blocks, into, side):
            src = xs[p].at[0, i2, blocks, :, pl.ds(0, sizes[p])]
            return go(src, f3[p].at[into, blocks], nb(DIMS[p][2], side))

        far = near(a2, 2)
        fw3[p][0] = (forward3(far, pl.ds(0, 2), 0, 1), forward3(far, pl.ds(2, 2), 0, -1))
        for k in (1, 2):
            fw3[p][k] = forward3(near(a2, roffs[k]), pl.ds(0, 4), k, side_of(k))
        for k in range(4):
            fw3[p][4 + k] = forward3(a2, near(a1, roffs[k]), 3, side_of(k))

    to_side = {1: [[None] * 8 for _ in range(3)], -1: [[None] * 8 for _ in range(3)]}
    back3 = {1: r3p, -1: r3m}
    sides = ((1, 1, 2), (-1, 2, 1))

    def line_to(p, side, which, k, added):
        value = tmp[p][which - 1, near(place(p)[1], roffs[k])]
        if added:
            fw3[p][k].wait_recv()
            value = value + f3[p][k].reshape(64, sizes[p]).astype(F32)
        put(p, which, k, value)
        to_side[side][p][k] = send3(p, which, k, pl.ds(0, 4), back3[side], side)

    for p in (1, 2, 0):
        for side, which, joined in sides:
            down(p, near(place(p)[2], side), tmp[p].at[which - 1])
            line_to(p, side, which, 3 - joined, False)
    for p in (1, 2, 0):
        for side, which, joined in sides:
            fw3[p][0][which - 1].wait_recv()
            value = tmp[p][which - 1, near(place(p)[1], 2)]
            added = f3[p][0, pl.ds(2 * which - 2, 2)].reshape(32, sizes[p]).astype(F32)
            if side == 1:
                value = jnp.concatenate([value[:32] + added, value[32:]], axis=0)
            else:
                value = jnp.concatenate([value[:32], value[32:] + added], axis=0)
            put(p, which, 0, value)
            to_side[side][p][0] = send3(p, which, 0, pl.ds(0, 4), back3[side], side)
    mig_a = x_second(va1, va2, ua, mig_a)
    mig_b = y_second(yb1, yb2, zb1, zb2, sb, mig_b)
    for p in (1, 2, 0):
        for side, which, joined in sides:
            line_to(p, side, which, joined, True)
    for p in (1, 2, 0):
        a1, a2, a3 = place(p)
        for k in range(4):
            i1 = near(a1, roffs[k])
            for side, which, joined in sides:
                value = tmp[p][which - 1, a2, pl.ds(pl.multiple_of(i1 * 16, 16), 16), :]
                if side_of(k) == side:
                    fw3[p][4 + k].wait_recv()
                    value = value + f3[p][3, i1].astype(F32)
                put_block(p, which, 3, i1, value)
                to_side[side][p][4 + k] = send3(p, which, 3, i1, back3[side], side)
    for p in (1, 2, 0):
        down(p, place(p)[2], t2[p])

    def settle(p, k):
        i2 = near(place(p)[1], roffs[k])
        to_side[1][p][k].wait_recv()
        to_side[-1][p][k].wait_recv()
        got = r3p[p][k].reshape(64, sizes[p]).astype(F32) + r3m[p][k].reshape(64, sizes[p]).astype(F32)
        t2[p][i2] = t2[p][i2] + got

    def t2_block(p, k, i1):
        return t2[p][near(place(p)[1], roffs[k]), pl.ds(pl.multiple_of(i1 * 16, 16), 16), :]

    def send2(p, which, i1, side):
        return go(s2[p].at[which, i1], q2[p].at[which, i1], nb(DIMS[p][1], side))

    fw2 = [[None] * 4 for _ in range(3)]
    for p in (1, 2, 0):
        settle(p, 0)
        for k in range(4):
            i1 = near(place(p)[0], roffs[k])
            s2[p][0, i1] = t2_block(p, 0, i1).astype(BF16)
            fw2[p][k] = send2(p, 0, i1, side_of(k))
    back2 = [[[None] * 4, [None] * 4] for _ in range(3)]
    for p in (1, 2, 0):
        settle(p, 1)
        settle(p, 2)
        for k in range(4):
            i1 = near(place(p)[0], roffs[k])
            fw2[p][k].wait_recv()
            for slot, side, line in ((1, 1, 2), (2, -1, 1)):
                value = t2_block(p, line, i1)
                if side_of(k) == side:
                    value = value + q2[p][0, i1].astype(F32)
                s2[p][slot, i1] = value.astype(BF16)
                back2[p][slot - 1][k] = send2(p, slot, i1, side)

    def settle_block(p, k):
        i1 = near(place(p)[0], roffs[k])
        to_side[1][p][4 + k].wait_recv()
        to_side[-1][p][4 + k].wait_recv()
        value = t2_block(p, 3, i1) + r3p[p][3, i1].astype(F32) + r3m[p][3, i1].astype(F32)
        back2[p][0][k].wait_recv()
        back2[p][1][k].wait_recv()
        return value + q2[p][1, i1].astype(F32) + q2[p][2, i1].astype(F32)

    sent1 = [[None] * 3 for _ in range(3)]
    for k, slot, delta in ((0, 0, 2), (1, 2, -1), (2, 1, 1)):
        for p in (1, 2, 0):
            s1[p][slot] = settle_block(p, k).astype(BF16)
            sent1[p][slot] = go(s1[p].at[slot], q1[p].at[slot], nb(DIMS[p][0], delta))

    def out_rows(part):
        return inc_ref.at[pl.ds(part * sub, sub), :]

    x_end(va1, va2, mig_a, out_rows(0), out_rows(1))
    y_end(zb1, zb2, mig_b, out_rows(2), out_rows(3))

    for p in (1, 2, 0):
        total = settle_block(p, 3)
        for slot in range(3):
            sent1[p][slot].wait_recv()
            total = total + q1[p][slot].astype(F32)
        fin[:, pl.ds(starts[p], sizes[p])] = total
    last = go(fin.at[pl.ds(pl.multiple_of(8 * oc, 8), 8), :], finr, sibling)
    routed_ref[:, mine] = fin[pl.ds(pl.multiple_of(8 * c, 8), 8), :].astype(BF16)
    last.wait_recv()
    routed_ref[:, other] = finr[...].astype(BF16)
    done_sending()


def finish(a_ref, b_ref, c_ref, x_ref, y_ref, z_ref):
    x_ref[...] = a_ref[...]
    y_ref[...] = b_ref[...]
    z_ref[...] = c_ref[...]


def body(hidden_in, routes, gates, gate_proj, up_proj, down_proj, query, kv_cache, lengths, moving, pair_mask):
    tokens, width = hidden_in.shape
    half = width // 2
    sizes = part_sizes(half)
    ff = gate_proj.shape[2]
    kv_cache, query = jnp.swapaxes(kv_cache, 1, 2), jnp.swapaxes(query, 1, 2)
    requests, kvw, slots = kv_cache.shape
    heads = query.shape[2]
    sub = kvw // 4

    def per_part(*lead, dtype=BF16, extra=False):
        return [
            pltpu.VMEM((*lead, s + (GATE_TILE if extra and p == GATE_PART else 0)), dtype)
            for p, s in enumerate(sizes)
        ]

    mig = (
        [pltpu.VMEM((2, sub, slots), BF16)] * 8
    )
    scratch = [
        *per_part(4, 4, 4, 16, extra=True),
        pltpu.VMEM((half, 4 * ff), BF16),
        pltpu.VMEM((2, ff, half), BF16),
        pltpu.VMEM((4, 4, 4, 16, 4 * ff), F32),
        pltpu.VMEM((4, 4, 4, 16, 2 * ff), F32),
        pltpu.VMEM((2, 4, 4, 4, 16, ff), BF16),
        pltpu.VMEM((2, 4, 4, 4, 16, GATE_TILE), F32),
        *per_part(2, 4, 64, dtype=F32),
        *per_part(4, 4, 16),
        *per_part(4, 4, 16),
        *per_part(4, 4, 16),
        *per_part(4, 64, dtype=F32),
        *per_part(3, 4, 16),
        *per_part(3, 4, 16),
        *per_part(3, 16),
        *per_part(3, 16),
        pltpu.VMEM((8, half + GATE_TILE), BF16),
        pltpu.VMEM((8, half + GATE_TILE), BF16),
        pltpu.VMEM((16, half), F32),
        pltpu.VMEM((8, half), F32),
        pltpu.VMEM((requests, kvw, slots), BF16),
        pltpu.VMEM((requests, kvw, heads), BF16),
        *mig,
        *mig,
        pltpu.SemaphoreType.DMA((272,)),
        pltpu.SemaphoreType.DMA((272,)),
        pltpu.SemaphoreType.DMA((8,)),
    ]
    vmem = pl.BlockSpec(memory_space=pltpu.VMEM)
    smem = pl.BlockSpec(memory_space=pltpu.SMEM)
    anywhere = pl.BlockSpec(memory_space=pl.ANY)
    routed, attention, incoming = pl.pallas_call(
        kernel,
        out_shape=(
            jax.ShapeDtypeStruct((tokens, width), BF16),
            jax.ShapeDtypeStruct((requests, heads, LAT), BF16),
            jax.ShapeDtypeStruct((kvw, slots), BF16),
        ),
        in_specs=[vmem, vmem, vmem, anywhere, anywhere, anywhere, anywhere, anywhere, smem, smem, smem],
        out_specs=(vmem, vmem, vmem),
        scratch_shapes=scratch,
        compiler_params=pltpu.CompilerParams(
            collective_id=0, has_side_effects=True, vmem_limit_bytes=64 * 1024 * 1024
        ),
        cost_estimate=pl.CostEstimate(flops=13_000_000_000, bytes_accessed=20_000_000, transcendentals=800_000),
    )(
        hidden_in, routes, gates, gate_proj[0], up_proj[0], down_proj[0], query, kv_cache, lengths, moving, pair_mask
    )
    results = (routed, attention, incoming)
    routed, attention, incoming = pl.pallas_call(
        finish,
        out_shape=tuple(jax.ShapeDtypeStruct(v.shape, v.dtype) for v in results),
        in_specs=[vmem] * 3,
        out_specs=(vmem,) * 3,
    )(*results)
    return routed, attention, incoming.T[None]


def solution(mesh):
    return jax.shard_map(
        body,
        mesh=mesh,
        in_specs=(
            P(("rank", "expert"), None),
            P(("rank", "expert"), None),
            P(("rank", "expert"), None),
            P("expert", None, "rank"),
            P("expert", None, "rank"),
            P("expert", "rank", None),
            P(("rank", "expert"), None, None),
            P(("rank", "expert"), None, None),
            P(("rank", "expert")),
            P(("rank", "expert")),
            P(),
        ),
        out_specs=(
            P(("rank", "expert"), None),
            P(("rank", "expert"), None, None),
            P(("rank", "expert"), None, None),
        ),
        check_vma=False,
    )
```

```python
import functools

import jax
import jax.numpy as jnp
from jax import lax
from jax.experimental import pallas as pl
from jax.experimental.pallas import tpu as pltpu
from jax.sharding import PartitionSpec as P

LAT = 512
SCALE = 192.0 ** (-0.5)
MESH = pl.DeviceIdType.MESH
F32 = jnp.float32
BF16 = jnp.bfloat16
GATE_TILE = 128

DIMS = ((1, 0, 2), (2, 1, 0), (0, 2, 1))
GATE_PART = 2


def part_sizes(half):
    if half == 3584:
        return (1536, 1024, 1024)
    return (half // 3,) * 3


def kernel(
    hid_ref, routes_ref, gates_ref, wg_ref, wu_ref, wd_ref, q_ref, kv_ref, len_ref, mov_ref, mask_ref,
    routed_ref, att_ref, inc_ref,
    x0, x1, x2, w, dn, acc, rb, h, gbuf, tmp0, tmp1, tmp2,
    f3_0, f3_1, f3_2, r3p_0, r3p_1, r3p_2, r3m_0, r3m_1, r3m_2, t2_0, t2_1, t2_2,
    s2_0, s2_1, s2_2, q2_0, q2_1, q2_2, s1_0, s1_1, s1_2, q1_0, q1_1, q1_2,
    stage_s, stage_r, fin, finr, kvv, qv,
    ya1, ya2, za1, za2, va1, va2, ua, sa, yb1, yb2, zb1, zb2, vb1, vb2, ub, sb,
    send_sems, recv_sems, local_sems,
):
    half = hid_ref.shape[1] // 2
    sizes = part_sizes(half)
    starts = (0, sizes[0], sizes[0] + sizes[1])
    xs, f3, r3p, r3m = (x0, x1, x2), (f3_0, f3_1, f3_2), (r3p_0, r3p_1, r3p_2), (r3m_0, r3m_1, r3m_2)
    tmp = (tmp0, tmp1, tmp2)
    t2, s2, q2 = (t2_0, t2_1, t2_2), (s2_0, s2_1, s2_2), (q2_0, q2_1, q2_2)
    s1, q1 = (s1_0, s1_1, s1_2), (q1_0, q1_1, q1_2)
    ff = wg_ref.shape[1]

    r = lax.axis_index("rank")
    e = lax.axis_index("expert")
    c = e % 2
    oc = 1 - c
    y = r % 4
    z = e // 4
    x = (r // 4) * 2 + (e // 2) % 2
    pos = (x, y, z)

    def at_chip(px, py, pz, core):
        return ((px // 2) * 4 + py, pz * 4 + (px % 2) * 2 + core)

    def nb(dim, delta):
        moved = [(v + delta + 4) % 4 if i == dim else v for i, v in enumerate(pos)]
        return at_chip(*moved, c)

    sibling = at_chip(x, y, z, oc)
    y_one = at_chip(x, y + 1 - 2 * (y % 2), z, c)
    y_three = at_chip(x, 3 - y, z, c)

    counter = [0]
    started = []

    def rc(src, dst, device):
        i = counter[0]
        counter[0] += 1
        return pltpu.make_async_remote_copy(
            src_ref=src, dst_ref=dst, send_sem=send_sems.at[i], recv_sem=recv_sems.at[i],
            device_id=device, device_id_type=MESH,
        )

    def go(src, dst, device):
        d = rc(src, dst, device)
        d.start()
        started.append(d)
        return d

    def done_sending():
        for d in started:
            d.wait_send()
        started.clear()

    locals_ = []

    def lc(src, dst):
        d = pltpu.make_async_copy(src, dst, local_sems.at[len(locals_)])
        locals_.append(d)
        d.start()
        return d

    lkv = lc(kv_ref, kvv)
    lq = lc(q_ref, qv)
    mine = pl.ds(pl.multiple_of(c * half, 128), half)
    other = pl.ds(pl.multiple_of(oc * half, 128), half)

    lane = lax.broadcasted_iota(jnp.int32, (8, GATE_TILE), 1)
    gate_rows = jnp.zeros((8, GATE_TILE), F32)
    wide_gates = gates_ref[...].astype(F32)
    names = routes_ref[...]
    for k in range(routes_ref.shape[1]):
        gate_rows = gate_rows + jnp.where(lane == names[:, k : k + 1], wide_gates[:, k : k + 1], 0.0)
    stage_s[:, pl.ds(0, half)] = hid_ref[:, other]
    stage_s[:, pl.ds(half, GATE_TILE)] = gate_rows.astype(BF16)

    barrier = pltpu.get_barrier_semaphore()
    for device in [nb(dim, delta) for dim in range(3) for delta in (1, -1, 2)] + [sibling]:
        pl.semaphore_signal(barrier, inc=1, device_id=device, device_id_type=MESH)
    pl.semaphore_wait(barrier, 10)

    tok = go(stage_s, stage_r, sibling)
    tok.wait_recv()
    cf = c.astype(F32)
    own_wide = jnp.concatenate([hid_ref[:, mine].astype(F32), gate_rows], axis=1)
    got_wide = stage_r[...].astype(F32)
    top = own_wide * (1.0 - cf) + got_wide * cf
    bottom = got_wide * (1.0 - cf) + own_wide * cf
    block = jnp.concatenate([top, bottom], axis=0).astype(BF16)

    def place(p):
        return tuple(pos[d] for d in DIMS[p])

    def near(v, delta):
        return (v + delta + 4) % 4

    for p in range(3):
        a1, a2, a3 = place(p)
        end = half + GATE_TILE if p == GATE_PART else starts[p] + sizes[p]
        xs[p][a3, a2, a1] = block[:, starts[p] : end]

    offs = (0, -1, 1, 2)

    def both_ways(ref, dim):
        return go(ref, ref, nb(dim, 1)), go(ref, ref, nb(dim, -1))

    g1, g2, g3 = [], [[None] * 4 for _ in range(3)], [[None] * 4 for _ in range(3)]
    own3 = [[None] * 4 for _ in range(3)]

    def block_at(p, k):
        a1, a2, a3 = place(p)
        return xs[p].at[a3, a2, near(a1, offs[k])]

    def second(p, k):
        g2[p][k] = both_ways(block_at(p, k), DIMS[p][1])

    def third_own(p, k):
        own3[p][k] = both_ways(block_at(p, k), DIMS[p][2])

    def third_line(p, k):
        a1, a2, a3 = place(p)
        g3[p][k] = both_ways(xs[p].at[a3, near(a2, offs[k])], DIMS[p][2])

    def side_of(k):
        return 1 if k % 2 == 0 else -1

    for p in range(3):
        g1.append(both_ways(block_at(p, 0), DIMS[p][0]))
    for p in range(3):
        second(p, 0)
    for p in range(3):
        third_own(p, 0)

    gate_cols = pl.ds(pl.multiple_of(2 * c * ff, 128), ff)
    up_cols = pl.ds(pl.multiple_of((2 * c + 1) * ff, 128), ff)
    lwg = lc(wg_ref.at[mine, :], w.at[:, gate_cols])
    lwu = lc(wu_ref.at[mine, :], w.at[:, up_cols])
    lwd = lc(wd_ref.at[:, mine], dn.at[c])
    rwg = go(wg_ref.at[other, :], w.at[:, gate_cols], sibling)
    rwu = go(wu_ref.at[other, :], w.at[:, up_cols], sibling)
    rwd = go(wd_ref.at[:, other], dn.at[c], sibling)

    mask = mask_ref[0]
    m_y = mask % 4
    m_x = mask // 4
    sub = ya1.shape[1]
    step_rows = 48 if sub % 48 == 0 else 16

    def for_rows(fn):
        @pl.loop(0, sub // step_rows)
        def _(i):
            fn(pl.ds(pl.multiple_of(i * step_rows, 16), step_rows))

    def pick_rows(dst, dst_slot, part):
        which = mov_ref[0]
        limit = len_ref[which]

        def one(rows):
            first = part * sub + rows.start
            piece = kvv[which, pl.ds(pl.multiple_of(first, 16), step_rows), :].astype(F32)
            at = lax.broadcasted_iota(jnp.int32, piece.shape, 1)
            dst[dst_slot, rows, :] = jnp.where(at < limit, piece, 0.0).astype(BF16)

        for_rows(one)

    def move_rows(dst, src, src_slot):
        def one(rows):
            dst[rows, :] = src[src_slot, rows, :]

        for_rows(one)

    def y_first(b1, b2):
        return go(b1.at[0], b1.at[1], y_one), go(b2.at[0], b2.at[1], y_three)

    def y_second(b1, b2, z1, z2, stage, first):
        first[0].wait_recv()
        first[1].wait_recv()
        move_rows(stage.at[0], b1, jnp.where(m_y == 3, 0, 1))
        s3 = go(stage.at[0], z1.at[1], y_three)
        move_rows(stage.at[1], b2, jnp.where(m_y == 1, 0, 1))
        s1_ = go(stage.at[1], z2.at[1], y_one)
        move_rows(z1.at[0], b1, jnp.where(m_y == 1, 1, 0))
        move_rows(z2.at[0], b2, jnp.where(m_y == 3, 1, 0))
        return s3, s1_

    def y_end(z1, z2, second, dst1, dst2):
        second[0].wait_recv()
        second[1].wait_recv()
        move_rows(dst1, z1, jnp.where(m_y <= 1, 0, 1))
        move_rows(dst2, z2, jnp.where((m_y == 0) | (m_y == 3), 0, 1))

    def x_first(v1, v2, u):
        return go(v1.at[0], u.at[0], nb(0, 1)), go(v2.at[0], u.at[1], nb(0, -1))

    def x_second(v1, v2, u, first):
        first[0].wait_recv()
        a = go(u.at[0], v1.at[1], nb(0, 1))
        first[1].wait_recv()
        return a, go(u.at[1], v2.at[1], nb(0, -1))

    def x_end(v1, v2, second, dst1, dst2):
        second[0].wait_recv()
        second[1].wait_recv()
        move_rows(dst1, v1, m_x)
        move_rows(dst2, v2, m_x)

    g1f = []
    for p in range(3):
        a1, a2, a3 = place(p)
        cut = xs[p].shape[4] // 256 * 128
        rest = xs[p].shape[4] - cut
        g1[p][0].wait_recv()
        left = xs[p].at[a3, a2, near(a1, -1), :, pl.ds(0, cut)]
        one = go(left, left, nb(DIMS[p][0], 1))
        g1[p][1].wait_recv()
        right = xs[p].at[a3, a2, near(a1, 1), :, pl.ds(cut, rest)]
        g1f.append((one, go(right, right, nb(DIMS[p][0], -1))))
    for p in range(3):
        second(p, 1)
        second(p, 2)
    for p in range(3):
        third_own(p, 1)
        third_own(p, 2)

    lq.wait()
    lkv.wait()

    def attend(b):
        kv = kvv[b]
        scores = lax.dot_general(qv[b], kv, (((0,), (0,)), ((), ())), preferred_element_type=F32) * SCALE
        valid = lax.broadcasted_iota(jnp.int32, scores.shape, 1) < len_ref[b]
        scores = jnp.where(valid, scores, -1e30)
        top_score = jnp.max(scores, axis=-1, keepdims=True)
        weights = jnp.where(valid, jnp.exp(scores - top_score), 0.0)
        total = jnp.sum(weights, axis=-1, keepdims=True)
        mixed = lax.dot_general(
            weights.astype(BF16), kv[:LAT, :], (((1,), (1,)), ((), ())), preferred_element_type=F32
        )
        att_ref[b] = (mixed / total).astype(BF16)

    g2f, own3f, g3f = ([[None] * 4 for _ in range(3)] for _ in range(3))

    def arrived(pair, k):
        pair[0 if k % 2 == 0 else 1].wait_recv()

    def rest_arrived(pair, k):
        pair[1 if k % 2 == 0 else 0].wait_recv()

    def second_on(p, k):
        a1, a2, a3 = place(p)
        arrived(g2[p][k], k)
        ref = xs[p].at[a3, near(a2, -side_of(k)), near(a1, offs[k])]
        g2f[p][k] = go(ref, ref, nb(DIMS[p][1], side_of(k)))

    def own_on(p, k):
        a1, a2, a3 = place(p)
        arrived(own3[p][k], k)
        ref = xs[p].at[near(a3, -side_of(k)), a2, near(a1, offs[k])]
        own3f[p][k] = go(ref, ref, nb(DIMS[p][2], side_of(k)))

    def line_on(p, k):
        a1, a2, a3 = place(p)
        arrived(g3[p][k], k)
        ref = xs[p].at[near(a3, -side_of(k)), near(a2, offs[k])]
        g3f[p][k] = (go(ref, ref, nb(DIMS[p][2], side_of(k))),)

    for p in range(3):
        second_on(p, 0)
    for p in range(3):
        own_on(p, 0)
    for p in range(3):
        g1f[p][0].wait_recv()
        g1f[p][1].wait_recv()
        second(p, 3)
    for p in range(3):
        third_own(p, 3)

    attend(0)

    for p in range(3):
        second_on(p, 1)
        second_on(p, 2)
    for p in range(3):
        own_on(p, 1)
        own_on(p, 2)

    @pl.loop(0, 4)
    def _(i):
        for j in range(4):
            acc[i, j] = jnp.zeros(acc.shape[2:], F32)

    for p in range(3):
        second_on(p, 3)
        for k in range(4):
            rest_arrived(g2[p][k], k)
        third_line(p, 1)
        third_line(p, 2)
    for p in range(3):
        own_on(p, 3)

    attend(1)

    for p in range(3):
        for k in range(4):
            g2f[p][k].wait_recv()
        third_line(p, 3)

    def rows_of(p, j):
        full = slice(None)
        if p == 0:
            return [(i, full, j) for i in range(4)]
        if p == 1:
            return [(j, i, full) for i in range(4)]
        return [(full, j, i) for i in range(4)]

    lwg.wait()
    lwu.wait()
    rwg.wait_recv()
    rwu.wait_recv()

    def index_of(p, i3, i2):
        full = slice(None)
        return ((i2, full, i3), (i3, i2, full), (full, i3, i2))[p]

    def project(p, lines):
        lhs = jnp.concatenate(
            [xs[p][i3, i2, :, :, : sizes[p]].reshape(64, sizes[p]) for i3, i2 in lines], axis=0
        )

        res = jnp.dot(lhs, w[pl.ds(starts[p], sizes[p]), :], preferred_element_type=F32)
        for i, line in enumerate(lines):
            at = index_of(p, *line)
            acc[at] = acc[at] + res[64 * i : 64 * i + 64].reshape(4, 16, 4 * ff)

    def lines_at(p, delta, which):
        a1, a2, a3 = place(p)
        return [(near(a3, delta), near(a2, offs[k])) for k in which]

    for p in range(3):
        line_on(p, 1)
        line_on(p, 2)
    pick_rows(ya1, 0, 0)
    pick_rows(ya2, 0, 1)
    mig_a = y_first(ya1, ya2)
    pick_rows(vb1, 0, 2)
    pick_rows(vb2, 0, 3)
    mig_b = x_first(vb1, vb2, ub)

    for p in range(3):
        project(p, lines_at(p, 0, range(4)))
    attend(2)
    for p in range(3):
        for k in range(4):
            rest_arrived(own3[p][k], k)
        rest_arrived(g3[p][1], 1)
        rest_arrived(g3[p][2], 2)
        project(p, lines_at(p, -1, range(3)) + lines_at(p, 1, range(3)))
    attend(3)
    for p in range(3):
        a1, a2, a3 = place(p)
        g3[p][3][0].wait_recv()
        left = xs[p].at[near(a3, -1), near(a2, 2), pl.ds(0, 2)]
        one = go(left, left, nb(DIMS[p][2], 1))
        g3[p][3][1].wait_recv()
        right = xs[p].at[near(a3, 1), near(a2, 2), pl.ds(2, 2)]
        g3f[p][3] = (one, go(right, right, nb(DIMS[p][2], -1)))
    mig_a = y_second(ya1, ya2, za1, za2, sa, mig_a)
    mig_b = x_second(vb1, vb2, ub, mig_b)
    for p in (1, 2, 0):
        for k in range(4):
            own3f[p][k].wait_recv()
        for k in (1, 2):
            g3f[p][k][0].wait_recv()
        project(p, lines_at(p, 2, range(3)) + lines_at(p, -1, (3,)) + lines_at(p, 1, (3,)))
    lwd.wait()
    rwd.wait_recv()
    for p in (1, 2, 0):
        for d in g3f[p][3]:
            d.wait_recv()
        project(p, lines_at(p, 2, (3,)))

    part_sends = []
    for k in (3, 1, 2, 0):
        xx = near(x, offs[k])
        part_sends.append(
            go(acc.at[xx, :, :, :, pl.ds(pl.multiple_of(2 * oc * ff, 128), 2 * ff)], rb.at[xx], sibling)
        )

    y_end(za1, za2, mig_a, va1.at[0], va2.at[0])
    mig_a = x_first(va1, va2, ua)
    x_end(vb1, vb2, mig_b, yb1.at[0], yb2.at[0])
    mig_b = y_first(yb1, yb2)

    for n in range(2):
        pick = lax.broadcasted_iota(jnp.int32, (GATE_TILE, GATE_TILE), 0) == e - c + n
        pick = jnp.where(pick, 1.0, 0.0).astype(BF16)
        for j in range(4):
            table = xs[GATE_PART][j][:, :, :, sizes[GATE_PART] :].reshape(256, GATE_TILE)
            spread = jnp.dot(table, pick, preferred_element_type=F32).reshape(4, 4, 16, GATE_TILE)
            for i, index in enumerate(rows_of(GATE_PART, j)):
                gbuf[(n, *index)] = spread[i]

    hid_sends = []
    for at, k in enumerate((3, 1, 2, 0)):
        xx = near(x, offs[k])
        part_sends[at].wait_recv()
        gate = acc[xx, :, :, :, gate_cols] + rb[xx, :, :, :, :ff]
        up = acc[xx, :, :, :, up_cols] + rb[xx, :, :, :, ff:]
        h[c, xx] = (gate * (1.0 / (1.0 + jnp.exp(-gate))) * up).astype(BF16)
        hid_sends.append(go(h.at[c, xx], h.at[c, xx], sibling))
    done_sending()

    def down(p, j, dst):
        def pull(ref, n):
            return jnp.concatenate([ref[(n, *i)].reshape(64, ref.shape[-1]) for i in rows_of(p, j)], axis=0)

        hs = [pull(h, n) for n in range(2)]
        gs = [pull(gbuf, n) for n in range(2)]
        most = sizes[p] if sizes[p] <= 1152 else sizes[p] // 2
        gs = [jnp.concatenate([g] * (most // GATE_TILE), axis=1) for g in gs]

        def tile(first, width):
            cols = pl.ds(pl.multiple_of(starts[p] + first, 128), width)
            out = gs[0][:, :width] * jnp.dot(hs[0], dn[0, :, cols], preferred_element_type=F32)
            out = out + gs[1][:, :width] * jnp.dot(hs[1], dn[1, :, cols], preferred_element_type=F32)
            at = pl.ds(pl.multiple_of(first, 128), width)
            if dst.dtype == BF16:
                dst[:, :, :, at] = out.astype(BF16).reshape(4, 4, 16, width)
            else:
                dst[:, :, at] = out.reshape(4, 64, width)

        for first in range(0, sizes[p], most):
            tile(first, most)

    roffs = (2, -1, 1, 0)

    def put(p, which, k2, value):
        xs[p][which, k2, :, :, : sizes[p]] = value.astype(BF16).reshape(4, 16, sizes[p])

    def put_block(p, which, k2, i1, value):
        xs[p][which, k2, i1, :, : sizes[p]] = value.astype(BF16)

    def send3(p, which, k2, blocks, into, side):
        src = xs[p].at[which, k2, blocks, :, pl.ds(0, sizes[p])]
        return go(src, into[p].at[k2, blocks], nb(DIMS[p][2], side))

    fw3 = [[None] * 8 for _ in range(3)]
    hid_sends[0].wait_recv()
    for p in (1, 0, 2):
        a1, a2, a3 = place(p)
        if p == 0:
            for d in hid_sends[1:]:
                d.wait_recv()
        down(p, near(a3, 2), xs[p].at[0])

        def forward3(i2, blocks, into, side):
            src = xs[p].at[0, i2, blocks, :, pl.ds(0, sizes[p])]
            return go(src, f3[p].at[into, blocks], nb(DIMS[p][2], side))

        far = near(a2, 2)
        fw3[p][0] = (forward3(far, pl.ds(0, 2), 0, 1), forward3(far, pl.ds(2, 2), 0, -1))
        for k in (1, 2):
            fw3[p][k] = forward3(near(a2, roffs[k]), pl.ds(0, 4), k, side_of(k))
        for k in range(4):
            fw3[p][4 + k] = forward3(a2, near(a1, roffs[k]), 3, side_of(k))

    to_side = {1: [[None] * 8 for _ in range(3)], -1: [[None] * 8 for _ in range(3)]}
    back3 = {1: r3p, -1: r3m}
    sides = ((1, 1, 2), (-1, 2, 1))

    def line_to(p, side, which, k, added):
        value = tmp[p][which - 1, near(place(p)[1], roffs[k])]
        if added:
            fw3[p][k].wait_recv()
            value = value + f3[p][k].reshape(64, sizes[p]).astype(F32)
        put(p, which, k, value)
        to_side[side][p][k] = send3(p, which, k, pl.ds(0, 4), back3[side], side)

    for p in (1, 2, 0):
        for side, which, joined in sides:
            down(p, near(place(p)[2], side), tmp[p].at[which - 1])
            line_to(p, side, which, 3 - joined, False)
    for p in (1, 2, 0):
        for side, which, joined in sides:
            fw3[p][0][which - 1].wait_recv()
            value = tmp[p][which - 1, near(place(p)[1], 2)]
            added = f3[p][0, pl.ds(2 * which - 2, 2)].reshape(32, sizes[p]).astype(F32)
            if side == 1:
                value = jnp.concatenate([value[:32] + added, value[32:]], axis=0)
            else:
                value = jnp.concatenate([value[:32], value[32:] + added], axis=0)
            put(p, which, 0, value)
            to_side[side][p][0] = send3(p, which, 0, pl.ds(0, 4), back3[side], side)
    mig_a = x_second(va1, va2, ua, mig_a)
    mig_b = y_second(yb1, yb2, zb1, zb2, sb, mig_b)
    for p in (1, 2, 0):
        for side, which, joined in sides:
            line_to(p, side, which, joined, True)
    for p in (1, 2, 0):
        a1, a2, a3 = place(p)
        for k in range(4):
            i1 = near(a1, roffs[k])
            for side, which, joined in sides:
                value = tmp[p][which - 1, a2, pl.ds(pl.multiple_of(i1 * 16, 16), 16), :]
                if side_of(k) == side:
                    fw3[p][4 + k].wait_recv()
                    value = value + f3[p][3, i1].astype(F32)
                put_block(p, which, 3, i1, value)
                to_side[side][p][4 + k] = send3(p, which, 3, i1, back3[side], side)
    for p in (1, 2, 0):
        down(p, place(p)[2], t2[p])

    def settle(p, k):
        i2 = near(place(p)[1], roffs[k])
        to_side[1][p][k].wait_recv()
        to_side[-1][p][k].wait_recv()
        got = r3p[p][k].reshape(64, sizes[p]).astype(F32) + r3m[p][k].reshape(64, sizes[p]).astype(F32)
        t2[p][i2] = t2[p][i2] + got

    def t2_block(p, k, i1):
        return t2[p][near(place(p)[1], roffs[k]), pl.ds(pl.multiple_of(i1 * 16, 16), 16), :]

    def send2(p, which, i1, side):
        return go(s2[p].at[which, i1], q2[p].at[which, i1], nb(DIMS[p][1], side))

    fw2 = [[None] * 4 for _ in range(3)]
    for p in (1, 2, 0):
        settle(p, 0)
        for k in range(4):
            i1 = near(place(p)[0], roffs[k])
            s2[p][0, i1] = t2_block(p, 0, i1).astype(BF16)
            fw2[p][k] = send2(p, 0, i1, side_of(k))
    back2 = [[[None] * 4, [None] * 4] for _ in range(3)]
    for p in (1, 2, 0):
        settle(p, 1)
        settle(p, 2)
        for k in range(4):
            i1 = near(place(p)[0], roffs[k])
            fw2[p][k].wait_recv()
            for slot, side, line in ((1, 1, 2), (2, -1, 1)):
                value = t2_block(p, line, i1)
                if side_of(k) == side:
                    value = value + q2[p][0, i1].astype(F32)
                s2[p][slot, i1] = value.astype(BF16)
                back2[p][slot - 1][k] = send2(p, slot, i1, side)

    def settle_block(p, k):
        i1 = near(place(p)[0], roffs[k])
        to_side[1][p][4 + k].wait_recv()
        to_side[-1][p][4 + k].wait_recv()
        value = t2_block(p, 3, i1) + r3p[p][3, i1].astype(F32) + r3m[p][3, i1].astype(F32)
        back2[p][0][k].wait_recv()
        back2[p][1][k].wait_recv()
        return value + q2[p][1, i1].astype(F32) + q2[p][2, i1].astype(F32)

    sent1 = [[None] * 3 for _ in range(3)]
    for k, slot, delta in ((0, 0, 2), (1, 2, -1), (2, 1, 1)):
        for p in (1, 2, 0):
            s1[p][slot] = settle_block(p, k).astype(BF16)
            sent1[p][slot] = go(s1[p].at[slot], q1[p].at[slot], nb(DIMS[p][0], delta))

    def out_rows(part):
        return inc_ref.at[pl.ds(part * sub, sub), :]

    x_end(va1, va2, mig_a, out_rows(0), out_rows(1))
    y_end(zb1, zb2, mig_b, out_rows(2), out_rows(3))

    for p in (1, 2, 0):
        total = settle_block(p, 3)
        for slot in range(3):
            sent1[p][slot].wait_recv()
            total = total + q1[p][slot].astype(F32)
        fin[:, pl.ds(starts[p], sizes[p])] = total
    last = go(fin.at[pl.ds(pl.multiple_of(8 * oc, 8), 8), :], finr, sibling)
    routed_ref[:, mine] = fin[pl.ds(pl.multiple_of(8 * c, 8), 8), :].astype(BF16)
    last.wait_recv()
    routed_ref[:, other] = finr[...].astype(BF16)
    done_sending()


def finish(a_ref, b_ref, c_ref, x_ref, y_ref, z_ref):
    x_ref[...] = a_ref[...]
    y_ref[...] = b_ref[...]
    z_ref[...] = c_ref[...]


def body(hidden_in, routes, gates, gate_proj, up_proj, down_proj, query, kv_cache, lengths, moving, pair_mask):
    tokens, width = hidden_in.shape
    half = width // 2
    sizes = part_sizes(half)
    ff = gate_proj.shape[2]
    kv_cache, query = jnp.swapaxes(kv_cache, 1, 2), jnp.swapaxes(query, 1, 2)
    requests, kvw, slots = kv_cache.shape
    heads = query.shape[2]
    sub = kvw // 4

    def per_part(*lead, dtype=BF16, extra=False):
        return [
            pltpu.VMEM((*lead, s + (GATE_TILE if extra and p == GATE_PART else 0)), dtype)
            for p, s in enumerate(sizes)
        ]

    mig = (
        [pltpu.VMEM((2, sub, slots), BF16)] * 8
    )
    scratch = [
        *per_part(4, 4, 4, 16, extra=True),
        pltpu.VMEM((half, 4 * ff), BF16),
        pltpu.VMEM((2, ff, half), BF16),
        pltpu.VMEM((4, 4, 4, 16, 4 * ff), F32),
        pltpu.VMEM((4, 4, 4, 16, 2 * ff), F32),
        pltpu.VMEM((2, 4, 4, 4, 16, ff), BF16),
        pltpu.VMEM((2, 4, 4, 4, 16, GATE_TILE), F32),
        *per_part(2, 4, 64, dtype=F32),
        *per_part(4, 4, 16),
        *per_part(4, 4, 16),
        *per_part(4, 4, 16),
        *per_part(4, 64, dtype=F32),
        *per_part(3, 4, 16),
        *per_part(3, 4, 16),
        *per_part(3, 16),
        *per_part(3, 16),
        pltpu.VMEM((8, half + GATE_TILE), BF16),
        pltpu.VMEM((8, half + GATE_TILE), BF16),
        pltpu.VMEM((16, half), F32),
        pltpu.VMEM((8, half), F32),
        pltpu.VMEM((requests, kvw, slots), BF16),
        pltpu.VMEM((requests, kvw, heads), BF16),
        *mig,
        *mig,
        pltpu.SemaphoreType.DMA((272,)),
        pltpu.SemaphoreType.DMA((272,)),
        pltpu.SemaphoreType.DMA((8,)),
    ]
    vmem = pl.BlockSpec(memory_space=pltpu.VMEM)
    smem = pl.BlockSpec(memory_space=pltpu.SMEM)
    anywhere = pl.BlockSpec(memory_space=pl.ANY)
    routed, attention, incoming = pl.pallas_call(
        kernel,
        out_shape=(
            jax.ShapeDtypeStruct((tokens, width), BF16),
            jax.ShapeDtypeStruct((requests, heads, LAT), BF16),
            jax.ShapeDtypeStruct((kvw, slots), BF16),
        ),
        in_specs=[vmem, vmem, vmem, anywhere, anywhere, anywhere, anywhere, anywhere, smem, smem, smem],
        out_specs=(vmem, vmem, vmem),
        scratch_shapes=scratch,
        compiler_params=pltpu.CompilerParams(
            collective_id=0, has_side_effects=True, vmem_limit_bytes=64 * 1024 * 1024
        ),
        cost_estimate=pl.CostEstimate(flops=13_000_000_000, bytes_accessed=20_000_000, transcendentals=800_000),
    )(
        hidden_in, routes, gates, gate_proj[0], up_proj[0], down_proj[0], query, kv_cache, lengths, moving, pair_mask
    )
    results = (routed, attention, incoming)
    routed, attention, incoming = pl.pallas_call(
        finish,
        out_shape=tuple(jax.ShapeDtypeStruct(v.shape, v.dtype) for v in results),
        in_specs=[vmem] * 3,
        out_specs=(vmem,) * 3,
    )(*results)
    return routed, attention, incoming.T[None]


def solution(mesh):
    return jax.shard_map(
        body,
        mesh=mesh,
        in_specs=(
            P(("rank", "expert"), None),
            P(("rank", "expert"), None),
            P(("rank", "expert"), None),
            P("expert", None, "rank"),
            P("expert", None, "rank"),
            P("expert", "rank", None),
            P(("rank", "expert"), None, None),
            P(("rank", "expert"), None, None),
            P(("rank", "expert")),
            P(("rank", "expert")),
            P(),
        ),
        out_specs=(
            P(("rank", "expert"), None),
            P(("rank", "expert"), None, None),
            P(("rank", "expert"), None, None),
        ),
        check_vma=False,
    )
```
